256 devices in a mesh: doc: 16 (over z, core), row: 4 (over x), col: 4 (over y).
Axes of the slice: x: 4, y: 4, z: 8, core: 2. Of those that a mesh axis runs over, the one named last changes fastest.
Arguments:
- tokens_in: bfloat16 [2048, 8192], P(('row', 'col'), 'doc'), may hold values from -6 to 6
- gate_weight: bfloat16 [8192, 14336], P('doc', ('row', 'col')), may hold values from -0.0625 to 0.0625
- up_weight: bfloat16 [8192, 14336], P('doc', ('row', 'col')), may hold values from -0.0625 to 0.0625
- doc_lengths: int32 [16, 8], P('doc'), may hold values from 1 to 64, 128 in all within a row
- subject_raw: int32 [16, 8], P('doc'), may hold values from 0 to 63
- residuals: bfloat16 [128, 8192], P(None, 'doc'), may hold values from -0.59765625 to 0.59765625
- regular: float32 [896], replicated, may hold values from 0.05 to 0.5
Outputs:
- panel_factor: float32 [14336, 896], P(('row', 'col'))
- updated_rhs: float32 [14336, 8192], P(('row', 'col'), 'doc')
The draws below stay inside these ranges and needn't reach their ends.
Inputs may be any that keep to these rules, and one draw needn't show every extreme that they name: `doc_lengths`: each group's lengths sum to 128; one of them is 64.
All inputs are finite; a program needn't handle non-finite values.
Results may differ from the reference program's by a relative error of at most 0.0041.
Values may be sent and summed in bfloat16 or wider, within the bound.
A program may use at most 128 MiB of HBM per device.

```python
import math
import jax
import jax.numpy as jnp
import numpy as np
from jax import lax

D = 8192
FFW = 14336
TOK_G = 128
DOCS_G = 8
GROUPS = 16
TOKENS = 2048
DOCS = 128
LONGEST = 64
PANEL = 896


def set_ends(drawn, stream_key, low, top_value):
    dims = drawn.shape
    place = [jax.random.randint(jax.random.fold_in(stream_key, axis), (), 0, dims[axis]) for axis in range(len(dims))]
    drawn = drawn.at[tuple(place)].set(low)
    longest = dims.index(max(dims))
    place[longest] = (place[longest] + 1) % dims[longest]
    return drawn.at[tuple(place)].set(top_value)


def steps_of(stream_key, shape, pieces, low, largest):
    def one(position, shards_of):
        steps = jax.random.uniform(jax.random.fold_in(jax.random.fold_in(stream_key, 6), position), (shards_of,), jnp.float32, low / len(pieces), largest / len(pieces))
        return jnp.repeat(jnp.exp(steps), shape[position] // shards_of).reshape((-1,) + (1,) * (len(shape) - position - 1))

    loudness = one(*pieces[0])
    for cut in pieces[1:]:
        loudness = loudness * one(*cut)
    return loudness


def split_up(amount, total, reach, skew):
    portions = [(1 << 20) // math.isqrt(grade ** skew) + 1 for grade in range(2, amount + 1)]
    spare, counts = total - reach - (amount - 1), [1] * (amount - 1)
    while spare > 0:
        candidates = [i for i in range(amount - 1) if counts[i] < reach]
        mass, remaining = sum([portions[i] for i in candidates]), spare
        for i in candidates:
            extra = min(reach - counts[i], max(1, remaining * portions[i] // mass), spare)
            counts[i] = counts[i] + extra
            spare = spare - extra
    return np.array([reach] + counts)


def uneven(rng, amount, total, reach, lean):
    if amount == 2:
        one = jax.random.randint(rng, (), max(1, total - reach), min(reach, total - 1) + 1)
        return jnp.stack([one, total - one])
    lengths = jnp.asarray(split_up(amount, total, reach, lean), jnp.int32)
    twos = (amount - 1) // 2
    donor, taker = lengths[1:1 + 2 * twos:2], lengths[2:2 + 2 * twos:2]
    margin = jnp.minimum(donor - 1, reach - taker)
    passed = jax.random.randint(jax.random.fold_in(rng, 1), (twos,), 0, 1 << 20) % (margin + 1)
    lengths = lengths.at[1:1 + 2 * twos:2].set(donor - passed).at[2:2 + 2 * twos:2].set(taker + passed)
    return lengths[jax.random.permutation(jax.random.fold_in(rng, 2), amount)]


def noise(rng, shape, width, limit, cuts=(), kind=jnp.bfloat16):
    result = width * jax.random.normal(rng, shape, jnp.float32)
    if cuts:
        result = result * steps_of(rng, shape, cuts, -0.22, 0.18)
    return jnp.clip(result, -limit, limit).astype(kind)


def setup_inputs(seed: int = 0) -> dict:
    splits = jax.random.split(jax.random.key(seed), 8)
    return {
        "tokens_in": noise(splits[0], (TOKENS, D), 1.0, 6.0, ((0, 16), (1, 16))),
        "gate_weight": noise(splits[1], (D, FFW), D ** -0.5, 0.0625, ((0, 16), (1, 16))),
        "up_weight": noise(splits[2], (D, FFW), D ** -0.5, 0.0625, ((0, 16), (1, 16))),
        "doc_lengths": jax.vmap(lambda own: uneven(own, DOCS_G, TOK_G, LONGEST, 2))(jax.random.split(splits[3], GROUPS)).reshape((GROUPS, DOCS_G)).astype(jnp.int32),
        "subject_raw": set_ends(jax.random.randint(splits[4], (GROUPS, DOCS_G), 0, LONGEST), jax.random.fold_in(splits[4], 1), 0, LONGEST - 1).astype(jnp.int32),
        "residuals": noise(splits[5], (DOCS, D), 0.1, 0.59765625, ((1, 16),)),
        "regular": jnp.clip(jnp.exp(jax.random.uniform(splits[6], (PANEL,), jnp.float32, math.log(0.05), math.log(0.5))), 0.05, 0.5),
    }


def reference(tokens_in, gate_weight, up_weight, doc_lengths, subject_raw, residuals, regular):
    gate_sum = jnp.dot(tokens_in.astype(jnp.float32), gate_weight.astype(jnp.float32), preferred_element_type=jnp.float32)
    up_sum = jnp.dot(tokens_in.astype(jnp.float32), up_weight.astype(jnp.float32), preferred_element_type=jnp.float32)
    key_rows = (jax.nn.silu(gate_sum) * up_sum).astype(jnp.bfloat16)
    offsets = (jnp.arange(GROUPS, dtype=jnp.int32) * TOK_G)[:, None]
    starts = jnp.cumsum(doc_lengths, axis=1, dtype=jnp.int32) - doc_lengths + offsets
    subject_spots = (starts + subject_raw % doc_lengths).reshape(-1).astype(jnp.int32)
    edit_keys = key_rows[subject_spots]
    gram_panel = jnp.dot(key_rows.T.astype(jnp.float32), key_rows[:, :PANEL].astype(jnp.float32), preferred_element_type=jnp.float32) / TOKENS
    edit_rhs = jnp.dot(edit_keys.T.astype(jnp.float32), residuals.astype(jnp.float32), preferred_element_type=jnp.float32)
    factor = jnp.linalg.cholesky(gram_panel[:PANEL] + jnp.diag(regular))
    lower_rows = jax.scipy.linalg.solve_triangular(factor, gram_panel[PANEL:].T, lower=True).T
    panel_solved = jax.scipy.linalg.solve_triangular(factor, edit_rhs[:PANEL], lower=True)
    rest_rows = edit_rhs[PANEL:] - jnp.dot(lower_rows, panel_solved, precision=lax.Precision.HIGHEST)
    panel_factor = jnp.concatenate([factor, lower_rows], axis=0)
    updated_rhs = jnp.concatenate([panel_solved, rest_rows], axis=0)
    return (panel_factor, updated_rhs)
```

```python
import functools
import math

import jax
import jax.numpy as jnp
from jax import lax
from jax.experimental import pallas as pl
from jax.experimental.pallas import tpu as pltpu
from jax.sharding import PartitionSpec as P

HI = lax.Precision.HIGHEST
MESH = pl.DeviceIdType.MESH
f32, bf16, i16, i32 = jnp.float32, jnp.bfloat16, jnp.int16, jnp.int32

ROWS, COLS, RING = 4, 4, 8
UNITS = 8
LN2 = math.log(2.0)
STEP = LN2 / 64
TOP = 32700.0


def dot(a, b, dims, precision=None):
    return lax.dot_general(a, b, (dims, ((), ())), precision=precision, preferred_element_type=f32)


def spread_row(v, k):
    return jnp.broadcast_to(v[k:k + 1, :], v.shape)


def spread_lane(v, j):
    return jnp.broadcast_to(v[:, j:j + 1], v.shape)


def factor_block(load, store):
    sub = lax.broadcasted_iota(jnp.int32, (8, 128), 0)
    lane = lax.broadcasted_iota(jnp.int32, (8, 128), 1)
    left = [load(i) for i in range(16)]
    right = [jnp.where(lane == sub + 8 * i, 1.0, 0.0).astype(f32) for i in range(16)]
    for p in range(16):
        cols = [spread_lane(left[p], 8 * p + k) for k in range(8)]
        below = {i: [spread_lane(left[i], 8 * p + k) for k in range(8)] for i in range(p + 1, 16)}
        pivots = jnp.zeros((8, 128), f32)
        a, v = left[p], right[p]
        for k in range(8):
            pivot = spread_row(cols[k], k)
            inv = 1.0 / pivot
            pivots = jnp.where(sub == k, pivot, pivots)
            ak, vk = spread_row(a, k), spread_row(v, k)
            lead = {m: spread_row(cols[m], k) for m in range(k + 1, 8)}
            mult = jnp.where(sub > k, cols[k] * inv, 0.0)
            for m in range(k + 1, 8):
                cols[m] = cols[m] - mult * lead[m]
            a = a - mult * ak
            v = v - mult * vk
            for i in range(p + 1, 16):
                part = below[i][k] * inv
                for m in range(k + 1, 8):
                    below[i][m] = below[i][m] - part * lead[m]
                left[i] = left[i] - part * ak
                right[i] = right[i] - part * vk
        scale = lax.rsqrt(pivots)
        store(p, jnp.where(lane >= sub + 8 * p, a * scale, 0.0), v * scale)


def chol_kernel(corner, regular, grams, edit0, edit, factor, rows_out, s_out, m, up, inv):
    n = corner.shape[0]
    blocks = n // 128
    r_i = lax.broadcasted_iota(jnp.int32, (128, 128), 0)
    c_i = lax.broadcasted_iota(jnp.int32, (128, 128), 1)
    m[...] = corner[...]
    for k in range(blocks):
        at = slice(k * 128, (k + 1) * 128)
        m[at, at] = m[at, at] + jnp.where(r_i == c_i, jnp.broadcast_to(regular[:, at], (128, 128)), 0.0)
    factor[...] = jnp.zeros((n, n), f32)

    def step(k, _):
        at = pl.ds(pl.multiple_of(k * 128, 128), 128)

        def load(i):
            return m[pl.ds(pl.multiple_of(k * 128 + 8 * i, 8), 8), at]

        def store(i, a, v):
            up[8 * i:8 * i + 8, :] = a
            inv[8 * i:8 * i + 8, :] = v

        factor_block(load, store)
        factor[at, at] = up[...].T
        for fixed in range(blocks):
            @pl.when(k == fixed)
            def _(fixed=fixed):
                lo, hi = fixed * 128, (fixed + 1) * 128
                li = inv[...]
                if fixed:
                    m[lo:hi, :lo] = dot(li, m[lo:hi, :lo], ((1,), (0,)), HI)
                m[lo:hi, lo:hi] = li
                if hi < n:
                    m[lo:hi, hi:] = dot(li, m[lo:hi, hi:], ((1,), (0,)), HI)
                    lt = m[lo:hi, hi:].T
                    factor[hi:, lo:hi] = lt
                    m[lo:hi, hi:] = m[lo:hi, hi:]
                    m[hi:, lo:hi] = jnp.zeros((n - hi, 128), f32)
                    for rlo in range(hi, n, 128):
                        m[rlo:rlo + 128, :] = m[rlo:rlo + 128, :] - dot(lt[rlo - hi:rlo - hi + 128], m[lo:hi, :], ((1,), (0,)), HI)
        return 0

    lax.fori_loop(0, blocks, step, 0)
    for k in range(blocks - 1):
        lo, hi = k * 128, (k + 1) * 128
        m[lo:hi, hi:] = jnp.zeros((128, n - hi), f32)
    l_rows = dot(grams[...], m[...], ((1,), (1,)), HI)
    s = dot(m[...], edit0[...], ((1,), (0,)), HI)
    s_out[...] = s
    rows_out[:, :n] = l_rows.astype(bf16)
    rows_out[:, n:] = (edit[...] - dot(l_rows, s, ((1,), (0,)), HI)).astype(bf16)


def chol_call(corner, regular, grams, edit0, edit):
    n = corner.shape[0]
    h, e = edit.shape
    return pl.pallas_call(
        chol_kernel,
        out_shape=[
            jax.ShapeDtypeStruct((n, n), f32),
            jax.ShapeDtypeStruct((h, n + e), bf16),
            jax.ShapeDtypeStruct((n, e), f32),
        ],
        scratch_shapes=[pltpu.VMEM((n, n), f32), pltpu.VMEM((128, 128), f32), pltpu.VMEM((128, 128), f32)],
        compiler_params=pltpu.CompilerParams(vmem_limit_bytes=48 << 20),
        name="panel_factor",
    )(corner, regular, grams, edit0, edit)

def place():
    doc = lax.axis_index("doc")
    return doc // 2, lax.rem(doc, 2), lax.axis_index("row"), lax.axis_index("col")


def at_device(z, core, row, col):
    return {"doc": z * 2 + core, "row": row, "col": col}


def greet(z, core, row, col, ring_steps):
    barrier = pltpu.get_barrier_semaphore()
    count = 0
    for dr in range(ROWS):
        for dc in range(COLS):
            for other in range(2):
                if dr == 0 and dc == 0 and other == 0:
                    continue
                device = at_device(z, lax.rem(core + other, 2), lax.rem(row + dr, ROWS), lax.rem(col + dc, COLS))
                pl.semaphore_signal(barrier, inc=1, device_id=device, device_id_type=MESH)
                count += 1
    for step in ring_steps:
        pl.semaphore_signal(barrier, inc=1, device_id=at_device(lax.rem(z + step, RING), core, row, col), device_id_type=MESH)
        count += 1
    return barrier, count


def remote(src, dst, send, recv, device):
    return pltpu.make_async_remote_copy(
        src_ref=src, dst_ref=dst, send_sem=send, recv_sem=recv, device_id=device, device_id_type=MESH
    )


def tile(start, size):
    return pl.ds(pl.multiple_of(start, size), size)


def project_kernel(tok, wg, wu, out, xg, wt, part, far_out, far_in, near_out, near_in,
                   xs, xr, ws, wr, fs, fr, ns, nr):
    z, core, row, col = place()
    depth, width = wg.shape
    piece = width // RING
    lanes = tok.shape[0]
    first = lax.rem(row, 2) * COLS + col
    mine = row // 2
    barrier, count = greet(z, core, row, col, (1, RING - 1))
    pl.semaphore_wait(barrier, count)

    def token_copy(i, half):
        spot = lax.rem(first - i + UNITS, UNITS)
        return remote(
            tok, xg.at[first, core], xs.at[2 * i + half], xr.at[first, core],
            at_device(z, mine, spot // COLS + 2 * half, lax.rem(spot, COLS)),
        )

    for i in range(UNITS):
        for half in range(2):
            if i == 0:
                @pl.when(jnp.logical_or(mine != half, core != mine))
                def _(i=i, half=half):
                    token_copy(i, half).start()
            else:
                token_copy(i, half).start()

    @pl.when(core == mine)
    def _():
        xg[first, core] = tok[...]

    partner = at_device(z, 1 - core, row, col)

    def weight_copy(j):
        rows = tile(j * 128, 128)
        return remote(wt.at[core, rows], wt.at[core, rows], ws.at[j], wr.at[j], partner)

    tiles = width // 128

    def turn(j, _):
        at = tile(j * 128, 128)
        wt[core, at, :] = wg[:, at].T
        weight_copy(j).start()
        wt[core, tile((j + tiles) * 128, 128), :] = wu[:, at].T
        weight_copy(j + tiles).start()
        return 0

    lax.fori_loop(0, tiles, turn, 0)

    def spot_of(u):
        return lax.rem(u + first, UNITS)

    def wait_tokens(u):
        for half in range(2):
            @pl.when(jnp.logical_not(jnp.logical_and(spot_of(u) == first, jnp.logical_and(half == core, core == mine))))
            def _(half=half):
                slot = xg.at[spot_of(u), half]
                remote(tok, slot, xs.at[0], xr.at[spot_of(u), half], partner).wait_recv()

    def project(pair):
        wait_tokens(2 * pair)
        wait_tokens(2 * pair + 1)
        x = [jnp.concatenate([xg[spot_of(2 * pair), half], xg[spot_of(2 * pair + 1), half]], axis=0) for half in range(2)]

        def chunk(j, _):
            rows = tile(j * 448, 448)
            total = dot(wt[0, rows, :], x[0], ((1,), (1,))) + dot(wt[1, rows, :], x[1], ((1,), (1,)))
            part[2 * pair, rows, :] = total[:, :lanes]
            part[2 * pair + 1, rows, :] = total[:, lanes:]
            return 0

        lax.fori_loop(0, 2 * width // 448, chunk, 0)

    def own(u, target):
        return (
            part[u, pl.ds(pl.multiple_of(target * piece, 16), piece), :],
            part[u, pl.ds(pl.multiple_of(width + target * piece, 16), piece), :],
        )

    def opened(slot):
        scale = jnp.exp(slot[2 * piece:, :].astype(i32).astype(f32)[:1] * STEP) * (1.0 / TOP)
        return (
            slot[:piece, :].astype(i32).astype(f32) * scale,
            slot[piece:2 * piece, :].astype(i32).astype(f32) * scale,
        )

    def packed(slot, g, v):
        top = jnp.maximum(jnp.max(jnp.abs(g), axis=0, keepdims=True), jnp.max(jnp.abs(v), axis=0, keepdims=True))
        grade = jnp.ceil(jnp.log(jnp.maximum(top, 1e-30)) * (1.0 / STEP)) + 1.0
        up = jnp.exp(grade * -STEP) * TOP
        slot[:piece, :] = jnp.round(g * up).astype(i32).astype(i16)
        slot[piece:2 * piece, :] = jnp.round(v * up).astype(i32).astype(i16)
        slot[2 * piece:, :] = jnp.broadcast_to(grade.astype(i32), (16, lanes)).astype(i16)

    def sign(u):
        return 1 - 2 * lax.rem(u, 2)

    def far(u, hop):
        return remote(far_out.at[u, hop], far_in.at[u, hop], fs.at[u, hop], fr.at[u, hop],
                      at_device(lax.rem(z + sign(u) + RING, RING), core, row, col))

    def near(u, hop):
        return remote(near_out.at[u, hop], near_in.at[u, hop], ns.at[u, hop], nr.at[u, hop],
                      at_device(lax.rem(z - sign(u) + RING, RING), core, row, col))

    def pass_on(u, hop):
        g, v = own(u, lax.rem(z + sign(u) * (4 - hop) + RING, RING))
        if hop:
            far(u, hop - 1).wait_recv()
            a, b = opened(far_in.at[u, hop - 1])
            g, v = g + a, v + b
        packed(far_out.at[u, hop], g, v)
        far(u, hop).start()
        if hop < 3:
            g, v = own(u, lax.rem(z - sign(u) * (3 - hop) + RING, RING))
            if hop:
                near(u, hop - 1).wait_recv()
                a, b = opened(near_in.at[u, hop - 1])
                g, v = g + a, v + b
            packed(near_out.at[u, hop], g, v)
            near(u, hop).start()

    def finish(u):
        g, v = own(u, z)
        near(u, 2).wait_recv()
        a, b = opened(near_in.at[u, 2])
        g, v = g + a, v + b
        far(u, 3).wait_recv()
        a, b = opened(far_in.at[u, 3])
        g, v = g + a, v + b
        out[:, tile(spot_of(u) * lanes, lanes)] = (g * (1.0 / (1.0 + jnp.exp(-g))) * v).astype(bf16)

    def weights_here(j, _):
        rows = tile(j * 128, 128)
        remote(wt.at[1 - core, rows], wt.at[1 - core, rows], ws.at[j], wr.at[j], partner).wait_recv()
        return 0

    lax.fori_loop(0, 2 * tiles, weights_here, 0)

    def step(g, _):
        for hop in range(1, 5):
            @pl.when(jnp.logical_and(g >= hop, g < UNITS + hop))
            def _(hop=hop):
                if hop < 4:
                    pass_on(g - hop, hop)
                else:
                    finish(g - hop)

        @pl.when(jnp.logical_and(lax.rem(g, 2) == 0, g < UNITS))
        def _():
            project(g // 2)

        @pl.when(g < UNITS)
        def _():
            pass_on(g, 0)
        return 0

    lax.fori_loop(0, UNITS + 4, step, 0)

    for i in range(UNITS):
        for half in range(2):
            if i == 0:
                @pl.when(jnp.logical_or(mine != half, core != mine))
                def _(i=i, half=half):
                    token_copy(i, half).wait_send()
            else:
                token_copy(i, half).wait_send()

    def sent(j, _):
        weight_copy(j).wait_send()
        return 0

    lax.fori_loop(0, 2 * tiles, sent, 0)

    def ring_sent(u, _):
        for hop in range(4):
            far(u, hop).wait_send()
            if hop < 3:
                near(u, hop).wait_send()
        return 0

    lax.fori_loop(0, UNITS, ring_sent, 0)


def project_call(tok, wg, wu):
    lanes, depth = tok.shape
    width = wg.shape[1]
    piece = width // RING
    rows = 2 * piece + 16
    return pl.pallas_call(
        project_kernel,
        out_shape=jax.ShapeDtypeStruct((piece, UNITS * lanes), bf16),
        in_specs=[pl.BlockSpec(memory_space=pltpu.VMEM)] * 3,
        out_specs=pl.BlockSpec(memory_space=pltpu.VMEM),
        scratch_shapes=[
            pltpu.VMEM((UNITS, 2, lanes, depth), bf16),
            pltpu.VMEM((2, 2 * width, depth), bf16),
            pltpu.VMEM((UNITS, 2 * width, lanes), f32),
            pltpu.VMEM((UNITS, 4, rows, lanes), i16),
            pltpu.VMEM((UNITS, 4, rows, lanes), i16),
            pltpu.VMEM((UNITS, 3, rows, lanes), i16),
            pltpu.VMEM((UNITS, 3, rows, lanes), i16),
            pltpu.SemaphoreType.DMA((2 * UNITS,)),
            pltpu.SemaphoreType.DMA((UNITS, 2)),
            pltpu.SemaphoreType.DMA((2 * width // 128,)),
            pltpu.SemaphoreType.DMA((2 * width // 128,)),
            pltpu.SemaphoreType.DMA((UNITS, 4)),
            pltpu.SemaphoreType.DMA((UNITS, 4)),
            pltpu.SemaphoreType.DMA((UNITS, 3)),
            pltpu.SemaphoreType.DMA((UNITS, 3)),
        ],
        compiler_params=pltpu.CompilerParams(collective_id=0, has_side_effects=True, vmem_limit_bytes=48 << 20),
        name="project_keys",
    )(tok, wg, wu)


def gram_kernel(keys, select, corner, grams, edit0, edit, k0, kb,
                ps, pr, ss, sr, zs, zr, xs, xr, hs, hr):
    z, core, row, col = place()
    piece = keys.shape[0]
    lanes = k0.shape[1] // (2 * UNITS)
    half_lanes = UNITS * lanes
    barrier, count = greet(z, core, row, col, tuple(range(1, RING)))
    pl.semaphore_wait(barrier, count)
    partner = at_device(z, 1 - core, row, col)
    mine = row // 2
    spot = lax.rem(row, 2) * COLS + col
    holder = core == mine
    origin = jnp.logical_and(row == 0, col == 0)
    own_rows = pl.ds(pl.multiple_of(z * piece, 16), piece)

    def block(c, t):
        return tile((c * UNITS + t) * lanes, lanes)

    def scatter(j):
        return remote(keys.at[:, pl.ds(j * lanes, lanes)], k0.at[own_rows, block(core, j)], ss.at[j], sr,
                      at_device(z, core, 2 * core + j // COLS, j % COLS))

    @pl.when(origin)
    def _():
        for j in range(UNITS):
            if j == 0:
                @pl.when(core == 1)
                def _():
                    scatter(0).start()
            else:
                scatter(j).start()

        @pl.when(core == 0)
        def _():
            k0[own_rows, :lanes] = keys[:, :lanes]

    own_half = tile(core * half_lanes, half_lanes)
    pair = remote(keys, kb.at[:, own_half], ps, pr, partner)
    pair.start()
    kb[:, own_half] = keys[...]

    def along(dz):
        here = k0.at[own_rows, block(core, spot)]
        return remote(here, here, zs.at[dz - 1], zr.at[dz - 1], at_device(lax.rem(z + dz, RING), core, row, col))

    def across(i):
        here = k0.at[:, block(core, spot)]
        return remote(here, here, xs.at[i - 1], xr.at[spot],
                      at_device(z, core, lax.rem(row + i // COLS, ROWS), lax.rem(col + i % COLS, COLS)))

    @pl.when(holder)
    def _():
        @pl.when(jnp.logical_not(jnp.logical_and(origin, core == 0)))
        def _():
            remote(keys.at[:, :lanes], k0.at[own_rows, block(core, spot)], ss.at[0], sr, partner).wait_recv()

        for dz in range(1, RING):
            along(dz).start()
        for dz in range(1, RING):
            there = k0.at[pl.ds(pl.multiple_of(lax.rem(z - dz + RING, RING) * piece, 16), piece), block(core, spot)]
            remote(there, there, zs.at[dz - 1], zr.at[dz - 1], partner).wait_recv()
        for i in range(1, ROWS * COLS):
            across(i).start()

    def hand_over(c, t):
        here = k0.at[:, block(c, t)]
        return remote(here, here, hs.at[t], hr.at[t], partner)

    for t in range(UNITS):
        @pl.when(jnp.logical_not(jnp.logical_and(holder, spot == t)))
        def _(t=t):
            here = k0.at[:, block(core, t)]
            remote(here, here, xs.at[0], xr.at[t], partner).wait_recv()
        hand_over(core, t).start()

    pair_in = remote(keys, kb.at[:, tile((1 - core) * half_lanes, half_lanes)], ps, pr, partner)
    pair_in.wait_recv()
    for t in range(UNITS):
        hand_over(1 - core, t).wait_recv()

    share = 1.0 / k0.shape[1]
    n = k0.shape[0]
    mid = n // 256 * 128 + 128
    nt = ((1,), (1,))
    grams[...] = dot(kb[...], k0[...], nt) * share
    corner[:mid, :] = dot(k0[:mid, :], k0[...], nt) * share
    corner[mid:, mid:] = dot(k0[mid:, :], k0[mid:, :], nt) * share
    corner[mid:, :mid] = jnp.zeros((n - mid, mid), f32)
    edit0[...] = dot(k0[...], select[...], ((1,), (0,)))
    edit[...] = dot(kb[...], select[...], ((1,), (0,)))

    pair.wait_send()
    for t in range(UNITS):
        hand_over(core, t).wait_send()

    @pl.when(origin)
    def _():
        for j in range(UNITS):
            if j == 0:
                @pl.when(core == 1)
                def _():
                    scatter(0).wait_send()
            else:
                scatter(j).wait_send()

    @pl.when(holder)
    def _():
        for dz in range(1, RING):
            along(dz).wait_send()
        for i in range(1, ROWS * COLS):
            across(i).wait_send()


def gram_call(keys, select):
    piece, half_lanes = keys.shape
    n, tokens = piece * RING, half_lanes * 2
    facts = select.shape[1]
    dma = pltpu.SemaphoreType.DMA
    return pl.pallas_call(
        gram_kernel,
        out_shape=[
            jax.ShapeDtypeStruct((n, n), f32),
            jax.ShapeDtypeStruct((piece, n), f32),
            jax.ShapeDtypeStruct((n, facts), f32),
            jax.ShapeDtypeStruct((piece, facts), f32),
        ],
        in_specs=[pl.BlockSpec(memory_space=pltpu.VMEM)] * 2,
        out_specs=[pl.BlockSpec(memory_space=pltpu.VMEM)] * 4,
        scratch_shapes=[
            pltpu.VMEM((n, tokens), bf16),
            pltpu.VMEM((piece, tokens), bf16),
            dma, dma, dma((UNITS,)), dma, dma((RING - 1,)), dma((RING - 1,)),
            dma((ROWS * COLS - 1,)), dma((UNITS,)), dma((UNITS,)), dma((UNITS,)),
        ],
        compiler_params=pltpu.CompilerParams(collective_id=1, has_side_effects=True, vmem_limit_bytes=48 << 20),
        name="gram_panel",
    )(keys, select)


def gather_kernel(rows, out, us, ur, ds, dr, hs, hr):
    z, core, row, col = place()
    piece, width = rows.shape
    half = width // 2
    barrier = pltpu.get_barrier_semaphore()
    partner = at_device(z, 1 - core, row, col)
    after = at_device(lax.rem(z + 1, RING), core, row, col)
    before = at_device(lax.rem(z + RING - 1, RING), core, row, col)
    for device in (partner, after, before):
        pl.semaphore_signal(barrier, inc=1, device_id=device, device_id_type=MESH)
    out[pl.ds(pl.multiple_of(z * piece, 16), piece), :] = rows[...]
    pl.semaphore_wait(barrier, 3)

    def slot(source, c, part=None):
        at = pl.ds(pl.multiple_of(lax.rem(source + 2 * RING, RING) * piece, 16), piece)
        if part is None:
            return out.at[at, tile(c * half, half)]
        return out.at[at, pl.ds(pl.multiple_of(c * half + part * (half // 2), half // 2), half // 2)]

    def upward(source, hop):
        here = slot(source, core, 0 if hop == 3 else None)
        return remote(here, here, us.at[hop], ur.at[hop], after)

    def downward(source, hop):
        here = slot(source, core, 1 if hop == 3 else None)
        return remote(here, here, ds.at[hop], dr.at[hop], before)

    def hand_over(source, c, index):
        here = slot(source, c)
        return remote(here, here, hs.at[index], hr.at[index], partner)

    upward(z, 0).start()
    downward(z, 0).start()
    for hop in range(1, 5):
        upward(z - hop, hop - 1).wait_recv()
        if hop < 4:
            upward(z - hop, hop).start()
        downward(z + hop, hop - 1).wait_recv()
        if hop < 4:
            downward(z + hop, hop).start()
            hand_over(z - hop, core, 2 * hop - 2).start()
            hand_over(z + hop, core, 2 * hop - 1).start()
        else:
            hand_over(z + hop, core, 6).start()
    for hop in range(1, 5):
        if hop < 4:
            hand_over(z - hop, 1 - core, 2 * hop - 2).wait_recv()
            hand_over(z + hop, 1 - core, 2 * hop - 1).wait_recv()
        else:
            hand_over(z + hop, 1 - core, 6).wait_recv()
    for hop in range(4):
        upward(z - hop, hop).wait_send()
        downward(z + hop, hop).wait_send()
    for hop in range(1, 5):
        if hop < 4:
            hand_over(z - hop, core, 2 * hop - 2).wait_send()
            hand_over(z + hop, core, 2 * hop - 1).wait_send()
        else:
            hand_over(z + hop, core, 6).wait_send()


def gather_call(rows):
    piece, width = rows.shape
    dma = pltpu.SemaphoreType.DMA
    return pl.pallas_call(
        gather_kernel,
        out_shape=jax.ShapeDtypeStruct((piece * RING, width), bf16),
        in_specs=[pl.BlockSpec(memory_space=pltpu.VMEM)],
        out_specs=pl.BlockSpec(memory_space=pltpu.VMEM),
        scratch_shapes=[dma((4,)), dma((4,)), dma((4,)), dma((4,)), dma((7,)), dma((7,))],
        compiler_params=pltpu.CompilerParams(collective_id=2, has_side_effects=True, vmem_limit_bytes=32 << 20),
        name="gather_rows",
    )(rows)


def on_device(tokens_in, gate_weight, up_weight, doc_lengths, subject_raw, residuals, regular):
    block_index = lax.axis_index(("row", "col"))
    both = lax.all_gather(jnp.concatenate([doc_lengths, subject_raw], axis=1), "doc", axis=0, tiled=True)
    groups, docs = both.shape[0], doc_lengths.shape[1]
    lengths, raw = both[:, :docs], both[:, docs:]
    tokens = tokens_in.shape[0] * ROWS * COLS
    offsets = lax.broadcasted_iota(i32, (groups, docs), 0) * (tokens // groups)
    starts = jnp.cumsum(lengths, axis=1, dtype=i32) - lengths + offsets
    spots = (starts + raw % lengths).reshape(1, -1)
    select = (lax.broadcasted_iota(i32, (tokens, groups * docs), 0) == spots).astype(bf16)
    keys = project_call(tokens_in, gate_weight, up_weight)
    corner, grams, edit0, edit = gram_call(keys, select)
    factor, rows, solved = chol_call(corner, regular.reshape(1, -1), grams, edit0, edit)
    full = gather_call(rows)
    n = factor.shape[0]
    l_block = jnp.where(block_index == 0, factor, full[:, :n].astype(f32))
    weight = jnp.where(block_index == 0, solved.astype(bf16), full[:, n:])
    updated = jnp.dot(weight, residuals, preferred_element_type=f32)
    return (l_block, updated)


def solution(mesh):
    return jax.shard_map(
        on_device,
        mesh=mesh,
        in_specs=(
            P(("row", "col"), "doc"),
            P("doc", ("row", "col")),
            P("doc", ("row", "col")),
            P("doc", None),
            P("doc", None),
            P(None, "doc"),
            P(),
        ),
        out_specs=(P(("row", "col"), None), P(("row", "col"), "doc")),
        check_vma=False,
    )
```

```python
import functools
import math

import jax
import jax.numpy as jnp
from jax import lax
from jax.experimental import pallas as pl
from jax.experimental.pallas import tpu as pltpu
from jax.sharding import PartitionSpec as P

HI = lax.Precision.HIGHEST
MESH = pl.DeviceIdType.MESH
f32, bf16, i16, i32 = jnp.float32, jnp.bfloat16, jnp.int16, jnp.int32

ROWS, COLS, RING = 4, 4, 8
UNITS = 8
LAG = 2
LN2 = math.log(2.0)
STEP = LN2 / 64
TOP = 32700.0


def dot(a, b, dims, precision=None):
    return lax.dot_general(a, b, (dims, ((), ())), precision=precision, preferred_element_type=f32)


def spread_row(v, k):
    return jnp.broadcast_to(v[k:k + 1, :], v.shape)


def spread_lane(v, j):
    return jnp.broadcast_to(v[:, j:j + 1], v.shape)


def factor_block(load, store):
    sub = lax.broadcasted_iota(jnp.int32, (8, 128), 0)
    lane = lax.broadcasted_iota(jnp.int32, (8, 128), 1)
    left = [load(i) for i in range(16)]
    right = [jnp.where(lane == sub + 8 * i, 1.0, 0.0).astype(f32) for i in range(16)]
    for p in range(16):
        cols = [spread_lane(left[p], 8 * p + k) for k in range(8)]
        below = {i: [spread_lane(left[i], 8 * p + k) for k in range(8)] for i in range(p + 1, 16)}
        pivots = jnp.zeros((8, 128), f32)
        a, v = left[p], right[p]
        for k in range(8):
            pivot = spread_row(cols[k], k)
            inv = 1.0 / pivot
            pivots = jnp.where(sub == k, pivot, pivots)
            ak, vk = spread_row(a, k), spread_row(v, k)
            lead = {m: spread_row(cols[m], k) for m in range(k + 1, 8)}
            mult = jnp.where(sub > k, cols[k] * inv, 0.0)
            for m in range(k + 1, 8):
                cols[m] = cols[m] - mult * lead[m]
            a = a - mult * ak
            v = v - mult * vk
            for i in range(p + 1, 16):
                part = below[i][k] * inv
                for m in range(k + 1, 8):
                    below[i][m] = below[i][m] - part * lead[m]
                left[i] = left[i] - part * ak
                right[i] = right[i] - part * vk
        scale = lax.rsqrt(pivots)
        store(p, jnp.where(lane >= sub + 8 * p, a * scale, 0.0), v * scale)


def place():
    doc = lax.axis_index("doc")
    return doc // 2, lax.rem(doc, 2), lax.axis_index("row"), lax.axis_index("col")


def at_device(z, core, row, col):
    return {"doc": z * 2 + core, "row": row, "col": col}


def greet(z, core, row, col, ring_steps):
    barrier = pltpu.get_barrier_semaphore()
    count = 0
    for dr in range(ROWS):
        for dc in range(COLS):
            for other in range(2):
                if dr == 0 and dc == 0 and other == 0:
                    continue
                device = at_device(z, lax.rem(core + other, 2), lax.rem(row + dr, ROWS), lax.rem(col + dc, COLS))
                pl.semaphore_signal(barrier, inc=1, device_id=device, device_id_type=MESH)
                count += 1
    for step in ring_steps:
        pl.semaphore_signal(barrier, inc=1, device_id=at_device(lax.rem(z + step, RING), core, row, col), device_id_type=MESH)
        count += 1
    return barrier, count


def remote(src, dst, send, recv, device):
    return pltpu.make_async_remote_copy(
        src_ref=src, dst_ref=dst, send_sem=send, recv_sem=recv, device_id=device, device_id_type=MESH
    )


def tile(start, size):
    return pl.ds(pl.multiple_of(start, size), size)


def project_kernel(tok_ref, wg_ref, wu_ref, docs, out, spots_out, tok, wg, wu, spots, xg, wt, part,
                   far_out, far_in, near_out, near_in,
                   ls, qs, qr, os, orr, xs, xr, ws, wr, fs, fr, ns, nr):
    z, core, row, col = place()
    loads = [pltpu.make_async_copy(a, b, ls.at[i]) for i, (a, b) in enumerate(((tok_ref, tok), (wg_ref, wg), (wu_ref, wu)))]
    for load in loads:
        load.start()
    depth, width = wg.shape
    piece = width // RING
    lanes = tok.shape[0]
    first = lax.rem(row, 2) * COLS + col
    mine = row // 2
    barrier, count = greet(z, core, row, col, tuple(range(1, RING)))
    sub = lax.broadcasted_iota(i32, (8, 128), 0)
    lengths = docs[:8, :].astype(f32)
    raw = docs[8:, :].astype(f32)
    starts = jnp.zeros((8, 128), f32)
    for j in range(7):
        starts = starts + jnp.where(sub > j, jnp.broadcast_to(lengths[j:j + 1, :], (8, 128)), 0.0)
    wrapped = raw - lengths * jnp.floor((raw + 0.5) / lengths)
    spots[core, z] = starts + wrapped + ((z * 2 + core) * lanes).astype(f32)
    pl.semaphore_wait(barrier, count)

    def spot_copy(dz):
        here = spots.at[core, z]
        return remote(here, here, qs.at[dz - 1], qr.at[dz - 1], at_device(lax.rem(z + dz, RING), core, row, col))

    loads[0].wait()

    def token_copy(i, half):
        spot = lax.rem(first - i + UNITS, UNITS)
        return remote(
            tok, xg.at[first, core], xs.at[2 * i + half], xr.at[first, core],
            at_device(z, mine, spot // COLS + 2 * half, lax.rem(spot, COLS)),
        )

    def start_tokens(waves):
        for i in waves:
            for half in range(2):
                if i == 0:
                    @pl.when(jnp.logical_or(mine != half, core != mine))
                    def _(i=i, half=half):
                        token_copy(i, half).start()
                else:
                    token_copy(i, half).start()

    start_tokens((0, 1))

    @pl.when(core == mine)
    def _():
        xg[first, core] = tok[...]

    partner = at_device(z, 1 - core, row, col)

    def weight_copy(j):
        rows = tile(j * 128, 128)
        return remote(wt.at[core, rows], wt.at[core, rows], ws.at[j], wr.at[j], partner)

    tiles = width // 128
    loads[1].wait()
    loads[2].wait()

    def turn(j, _):
        at = tile(j * 128, 128)
        wt[core, at, :] = wg[:, at].T
        weight_copy(j).start()
        wt[core, tile((j + tiles) * 128, 128), :] = wu[:, at].T
        weight_copy(j + tiles).start()
        return 0

    lax.fori_loop(0, tiles, turn, 0)
    start_tokens((2, 3))
    for dz in range(1, RING):
        spot_copy(dz).start()

    def spot_of(u):
        return lax.rem(u + first, UNITS)

    def wait_tokens(u):
        for half in range(2):
            @pl.when(jnp.logical_not(jnp.logical_and(spot_of(u) == first, jnp.logical_and(half == core, core == mine))))
            def _(half=half):
                slot = xg.at[spot_of(u), half]
                remote(tok, slot, xs.at[0], xr.at[spot_of(u), half], partner).wait_recv()

    def project(pair):
        wait_tokens(2 * pair)
        wait_tokens(2 * pair + 1)
        x = [jnp.concatenate([xg[spot_of(2 * pair), half], xg[spot_of(2 * pair + 1), half]], axis=0) for half in range(2)]

        def chunk(j, _):
            rows = tile(j * 448, 448)
            total = dot(wt[0, rows, :], x[0], ((1,), (1,))) + dot(wt[1, rows, :], x[1], ((1,), (1,)))
            part[2 * pair, rows, :] = total[:, :lanes]
            part[2 * pair + 1, rows, :] = total[:, lanes:]
            return 0

        lax.fori_loop(0, 2 * width // 448, chunk, 0)

    def own(u, target):
        return (
            part[u, pl.ds(pl.multiple_of(target * piece, 16), piece), :],
            part[u, pl.ds(pl.multiple_of(width + target * piece, 16), piece), :],
        )

    def opened(slot):
        scale = jnp.exp(slot[2 * piece:, :].astype(i32).astype(f32)[:1] * STEP) * (1.0 / TOP)
        return (
            slot[:piece, :].astype(i32).astype(f32) * scale,
            slot[piece:2 * piece, :].astype(i32).astype(f32) * scale,
        )

    def packed(slot, g, v):
        top = jnp.maximum(jnp.max(jnp.abs(g), axis=0, keepdims=True), jnp.max(jnp.abs(v), axis=0, keepdims=True))
        grade = jnp.ceil(jnp.log(jnp.maximum(top, 1e-30)) * (1.0 / STEP)) + 1.0
        up = jnp.exp(grade * -STEP) * TOP
        slot[:piece, :] = jnp.round(g * up).astype(i32).astype(i16)
        slot[piece:2 * piece, :] = jnp.round(v * up).astype(i32).astype(i16)
        slot[2 * piece:, :] = jnp.broadcast_to(grade.astype(i32), (16, lanes)).astype(i16)

    def sign(u):
        return 1 - 2 * lax.rem(u, 2)

    def far(u, hop):
        return remote(far_out.at[u, hop], far_in.at[u, hop], fs.at[u, hop], fr.at[u, hop],
                      at_device(lax.rem(z + sign(u) + RING, RING), core, row, col))

    def near(u, hop):
        return remote(near_out.at[u, hop], near_in.at[u, hop], ns.at[u, hop], nr.at[u, hop],
                      at_device(lax.rem(z - sign(u) + RING, RING), core, row, col))

    def pass_on(u, hop):
        g, v = own(u, lax.rem(z + sign(u) * (4 - hop) + RING, RING))
        if hop:
            far(u, hop - 1).wait_recv()
            a, b = opened(far_in.at[u, hop - 1])
            g, v = g + a, v + b
        packed(far_out.at[u, hop], g, v)
        far(u, hop).start()
        if hop < 3:
            g, v = own(u, lax.rem(z - sign(u) * (3 - hop) + RING, RING))
            if hop:
                near(u, hop - 1).wait_recv()
                a, b = opened(near_in.at[u, hop - 1])
                g, v = g + a, v + b
            packed(near_out.at[u, hop], g, v)
            near(u, hop).start()

    def finish(u):
        g, v = own(u, z)
        near(u, 2).wait_recv()
        a, b = opened(near_in.at[u, 2])
        g, v = g + a, v + b
        far(u, 3).wait_recv()
        a, b = opened(far_in.at[u, 3])
        g, v = g + a, v + b
        out[spot_of(u)] = (g * (1.0 / (1.0 + jnp.exp(-g))) * v).astype(bf16)

    def weights_here(j, _):
        rows = tile(j * 128, 128)
        remote(wt.at[1 - core, rows], wt.at[1 - core, rows], ws.at[j], wr.at[j], partner).wait_recv()
        return 0

    lax.fori_loop(0, 2 * tiles, weights_here, 0)

    def step(g, _):
        for hop in range(1, 5):
            @pl.when(jnp.logical_and(g >= LAG * hop, g < UNITS + LAG * hop))
            def _(hop=hop):
                if hop < 4:
                    pass_on(g - LAG * hop, hop)
                else:
                    finish(g - LAG * hop)

        @pl.when(jnp.logical_and(lax.rem(g, 2) == 0, g < UNITS))
        def _():
            project(g // 2)

        @pl.when(g < UNITS)
        def _():
            pass_on(g, 0)

        @pl.when(g == 0)
        def _():
            start_tokens((4, 5))

        @pl.when(g == 2)
        def _():
            start_tokens((6, 7))
        return 0

    lax.fori_loop(0, UNITS + 4 * LAG, step, 0)

    for dz in range(1, RING):
        there = spots.at[core, lax.rem(z - dz + RING, RING)]
        remote(there, there, qs.at[dz - 1], qr.at[dz - 1], partner).wait_recv()
    over = remote(spots.at[core], spots.at[core], os, orr, partner)
    over.start()
    remote(spots.at[1 - core], spots.at[1 - core], os, orr, partner).wait_recv()
    for group in range(2 * RING):
        spots_out[group * 8:(group + 1) * 8, :] = spots[group % 2, group // 2]
    over.wait_send()
    for dz in range(1, RING):
        spot_copy(dz).wait_send()

    for i in range(UNITS):
        for half in range(2):
            if i == 0:
                @pl.when(jnp.logical_or(mine != half, core != mine))
                def _(i=i, half=half):
                    token_copy(i, half).wait_send()
            else:
                token_copy(i, half).wait_send()

    def sent(j, _):
        weight_copy(j).wait_send()
        return 0

    lax.fori_loop(0, 2 * tiles, sent, 0)

    def ring_sent(u, _):
        for hop in range(4):
            far(u, hop).wait_send()
            if hop < 3:
                near(u, hop).wait_send()
        return 0

    lax.fori_loop(0, UNITS, ring_sent, 0)


def project_call(tok, wg, wu, docs):
    lanes, depth = tok.shape
    width = wg.shape[1]
    piece = width // RING
    rows = 2 * piece + 16
    return pl.pallas_call(
        project_kernel,
        out_shape=[jax.ShapeDtypeStruct((UNITS, piece, lanes), bf16), jax.ShapeDtypeStruct((16 * RING, 128), f32)],
        in_specs=[pl.BlockSpec(memory_space=pl.ANY)] * 3 + [pl.BlockSpec(memory_space=pltpu.VMEM)],
        out_specs=[pl.BlockSpec(memory_space=pltpu.VMEM)] * 2,
        scratch_shapes=[
            pltpu.VMEM((lanes, depth), bf16),
            pltpu.VMEM((depth, width), bf16),
            pltpu.VMEM((depth, width), bf16),
            pltpu.VMEM((2, RING, 8, 128), f32),
            pltpu.VMEM((UNITS, 2, lanes, depth), bf16),
            pltpu.VMEM((2, 2 * width, depth), bf16),
            pltpu.VMEM((UNITS, 2 * width, lanes), f32),
            pltpu.VMEM((UNITS, 4, rows, lanes), i16),
            pltpu.VMEM((UNITS, 4, rows, lanes), i16),
            pltpu.VMEM((UNITS, 3, rows, lanes), i16),
            pltpu.VMEM((UNITS, 3, rows, lanes), i16),
            pltpu.SemaphoreType.DMA((3,)),
            pltpu.SemaphoreType.DMA((RING - 1,)),
            pltpu.SemaphoreType.DMA((RING - 1,)),
            pltpu.SemaphoreType.DMA,
            pltpu.SemaphoreType.DMA,
            pltpu.SemaphoreType.DMA((2 * UNITS,)),
            pltpu.SemaphoreType.DMA((UNITS, 2)),
            pltpu.SemaphoreType.DMA((2 * width // 128,)),
            pltpu.SemaphoreType.DMA((2 * width // 128,)),
            pltpu.SemaphoreType.DMA((UNITS, 4)),
            pltpu.SemaphoreType.DMA((UNITS, 4)),
            pltpu.SemaphoreType.DMA((UNITS, 3)),
            pltpu.SemaphoreType.DMA((UNITS, 3)),
        ],
        compiler_params=pltpu.CompilerParams(collective_id=0, has_side_effects=True, vmem_limit_bytes=48 << 20),
        name="project_keys",
    )(tok, wg, wu, docs)


def factor_kernel(keys, spots, regular, factor, inv_hi, inv_lo, solved, g_all, e_all,
                  k0, kb, select, m, up, inv, grams, edit0, edit,
                  ps, pr, ss, sr, zs, zr, xs, xr, hs, hr, gs, gr, es, er, os, orr):
    z, core, row, col = place()
    piece, lanes = keys.shape[1:]
    n = k0.shape[1]
    tokens = 2 * UNITS * lanes
    barrier, count = greet(z, core, row, col, tuple(range(1, RING)))
    pl.semaphore_wait(barrier, count)
    partner = at_device(z, 1 - core, row, col)
    mine = row // 2
    spot = lax.rem(row, 2) * COLS + col
    holder = core == mine
    origin = jnp.logical_and(row == 0, col == 0)

    def rows_of(zz):
        return pl.ds(pl.multiple_of(zz * piece, 16), piece)

    def scatter(j):
        return remote(keys.at[j], k0.at[core * UNITS + j, rows_of(z)], ss.at[j], sr,
                      at_device(z, core, 2 * core + j // COLS, j % COLS))

    @pl.when(origin)
    def _():
        for j in range(UNITS):
            if j == 0:
                @pl.when(core == 1)
                def _():
                    scatter(0).start()
            else:
                scatter(j).start()

        @pl.when(core == 0)
        def _():
            k0[0, rows_of(z), :] = keys[0]

    pair = remote(keys, kb.at[pl.ds(core * UNITS, UNITS)], ps, pr, partner)
    pair.start()
    for j in range(UNITS):
        kb[core * UNITS + j] = keys[j]

    def along(dz):
        here = k0.at[core * UNITS + spot, rows_of(z)]
        return remote(here, here, zs.at[dz - 1], zr.at[dz - 1], at_device(lax.rem(z + dz, RING), core, row, col))

    def across(i):
        here = k0.at[core * UNITS + spot]
        return remote(here, here, xs.at[i - 1], xr.at[spot],
                      at_device(z, core, lax.rem(row + i // COLS, ROWS), lax.rem(col + i % COLS, COLS)))

    @pl.when(holder)
    def _():
        @pl.when(jnp.logical_not(jnp.logical_and(origin, core == 0)))
        def _():
            remote(keys.at[0], k0.at[core * UNITS + spot, rows_of(z)], ss.at[0], sr, partner).wait_recv()

        for dz in range(1, RING):
            along(dz).start()
        for dz in range(1, RING):
            there = k0.at[core * UNITS + spot, rows_of(lax.rem(z - dz + RING, RING))]
            remote(there, there, zs.at[dz - 1], zr.at[dz - 1], partner).wait_recv()
        for i in range(1, ROWS * COLS):
            across(i).start()

    lane = lax.broadcasted_iota(i32, (128, 128), 1)
    for b in range(2 * UNITS):
        select[b] = jnp.where(lane + b * lanes == spots[...].astype(i32), 1.0, 0.0).astype(bf16)
    m[...] = jnp.zeros((n, n), f32)
    grams[...] = jnp.zeros(grams.shape, f32)
    edit0[...] = jnp.zeros(edit0.shape, f32)
    edit[...] = jnp.zeros(edit.shape, f32)
    mid = n // 256 * 128 + 128
    nt = ((1,), (1,))

    def hand_over(c, t):
        here = k0.at[c * UNITS + t]
        return remote(here, here, hs.at[t], hr.at[t], partner)

    def add_pair(c, q):
        b = c * UNITS + 2 * q
        a = jnp.concatenate([k0[b], k0[b + 1]], axis=1)
        own = jnp.concatenate([kb[b], kb[b + 1]], axis=1)
        hot = jnp.concatenate([select[b], select[b + 1]], axis=1)
        m[:mid, :] = m[:mid, :] + dot(a[:mid], a, nt)
        m[mid:, mid:] = m[mid:, mid:] + dot(a[mid:], a[mid:], nt)
        grams[...] = grams[...] + dot(own, a, nt)
        edit0[...] = edit0[...] + dot(a, hot, nt)
        edit[...] = edit[...] + dot(own, hot, nt)

    remote(keys, kb.at[pl.ds((1 - core) * UNITS, UNITS)], ps, pr, partner).wait_recv()

    def near_pair(q, _):
        for j in range(2):
            t = 2 * q + j

            @pl.when(jnp.logical_not(jnp.logical_and(holder, spot == t)))
            def _():
                here = k0.at[core * UNITS + t]
                remote(here, here, xs.at[0], xr.at[t], partner).wait_recv()
            hand_over(core, t).start()
        add_pair(core, q)
        return 0

    lax.fori_loop(0, UNITS // 2, near_pair, 0)

    def far_pair(q, _):
        for j in range(2):
            hand_over(1 - core, 2 * q + j).wait_recv()
        add_pair(1 - core, q)
        return 0

    lax.fori_loop(0, UNITS // 2, far_pair, 0)

    share = 1.0 / tokens
    top = jnp.max(jnp.abs(grams[...]), axis=1, keepdims=True) * share
    grade = jnp.ceil(jnp.log(jnp.maximum(top, 1e-30)) * (1.0 / STEP)) + 1.0
    scaled = jnp.round(grams[...] * (jnp.exp(grade * -STEP) * (TOP * share))).astype(i32).astype(i16)
    half = g_all.shape[3]

    @pl.when(core == 0)
    def _():
        g_all[0, z] = scaled[:, :half]

    @pl.when(core == 1)
    def _():
        g_all[1, z, :, :n - half] = scaled[:, half:]
        g_all[1, z, :, n - half:] = jnp.broadcast_to(grade.astype(i32), (piece, 2 * half - n)).astype(i16)

    e_all[z] = edit[...].astype(bf16)

    def give(dz):
        there = at_device(lax.rem(z + dz, RING), core, row, col)
        g, e = g_all.at[core, z], e_all.at[z]
        return (remote(g, g, gs.at[dz - 1], gr.at[dz - 1], there), remote(e, e, es.at[dz - 1], er.at[dz - 1], there))

    def take(dz):
        source = lax.rem(z - dz + RING, RING)
        g, e = g_all.at[core, source], e_all.at[source]
        return (remote(g, g, gs.at[dz - 1], gr.at[dz - 1], partner), remote(e, e, es.at[dz - 1], er.at[dz - 1], partner))

    for dz in range(1, RING):
        for copy in give(dz):
            copy.start()
    over = remote(g_all.at[core], g_all.at[core], os, orr, partner)

    blocks = n // 128
    r_i = lax.broadcasted_iota(i32, (128, 128), 0)
    c_i = lax.broadcasted_iota(i32, (128, 128), 1)
    m[...] = m[...] * share
    for k in range(blocks):
        at = slice(k * 128, (k + 1) * 128)
        m[at, at] = m[at, at] + jnp.where(r_i == c_i, jnp.broadcast_to(regular[:, at], (128, 128)), 0.0)
    factor[...] = jnp.zeros((n, n), f32)

    def step(k, _):
        at = pl.ds(pl.multiple_of(k * 128, 128), 128)

        def load(i):
            return m[pl.ds(pl.multiple_of(k * 128 + 8 * i, 8), 8), at]

        def store(i, a, v):
            up[8 * i:8 * i + 8, :] = a
            inv[8 * i:8 * i + 8, :] = v

        factor_block(load, store)
        factor[at, at] = up[...].T

        @pl.when(k == blocks - 2)
        def _():
            for dz in range(1, RING):
                for copy in take(dz):
                    copy.wait_recv()
            over.start()

        for fixed in range(blocks):
            @pl.when(k == fixed)
            def _(fixed=fixed):
                lo, hi = fixed * 128, (fixed + 1) * 128
                li = inv[...]
                if fixed:
                    m[lo:hi, :lo] = dot(li, m[lo:hi, :lo], ((1,), (0,)), HI)
                m[lo:hi, lo:hi] = li
                if hi < n:
                    m[lo:hi, hi:] = dot(li, m[lo:hi, hi:], ((1,), (0,)), HI)
                    lt = m[lo:hi, hi:].T
                    factor[hi:, lo:hi] = lt
                    for rlo in range(hi, n, 128):
                        rows = slice(rlo, rlo + 128)
                        cut = lt[rlo - hi:rlo - hi + 128]
                        if fixed:
                            m[rows, :lo] = m[rows, :lo] - dot(cut, m[lo:hi, :lo], ((1,), (0,)), HI)
                        m[rows, lo:hi] = -dot(cut, li, ((1,), (0,)), HI)
                        m[rows, rlo:] = m[rows, rlo:] - dot(cut, m[lo:hi, rlo:], ((1,), (0,)), HI)
        return 0

    lax.fori_loop(0, blocks, step, 0)
    for k in range(blocks - 1):
        lo, hi = k * 128, (k + 1) * 128
        m[lo:hi, hi:] = jnp.zeros((128, n - hi), f32)
    solved[...] = dot(m[...], edit0[...], ((1,), (0,)), HI)
    whole, rest = split(m[...])
    inv_hi[...] = whole
    inv_lo[...] = rest

    remote(g_all.at[1 - core], g_all.at[1 - core], os, orr, partner).wait_recv()
    over.wait_send()
    for dz in range(1, RING):
        for copy in give(dz):
            copy.wait_send()
    pair.wait_send()
    for t in range(UNITS):
        hand_over(core, t).wait_send()

    @pl.when(origin)
    def _():
        for j in range(UNITS):
            if j == 0:
                @pl.when(core == 1)
                def _():
                    scatter(0).wait_send()
            else:
                scatter(j).wait_send()

    @pl.when(holder)
    def _():
        for dz in range(1, RING):
            along(dz).wait_send()
        for i in range(1, ROWS * COLS):
            across(i).wait_send()


def split(a):
    whole = a.astype(bf16)
    return whole, (a - whole.astype(f32)).astype(bf16)


def factor_call(keys, spots, regular):
    units, piece, lanes = keys.shape
    n, blocks = piece * RING, 2 * units
    facts = spots.shape[0]
    dma = pltpu.SemaphoreType.DMA
    vmem = pl.BlockSpec(memory_space=pltpu.VMEM)
    return pl.pallas_call(
        factor_kernel,
        out_shape=[
            jax.ShapeDtypeStruct((n, n), f32),
            jax.ShapeDtypeStruct((n, n), bf16),
            jax.ShapeDtypeStruct((n, n), bf16),
            jax.ShapeDtypeStruct((n, facts), f32),
            jax.ShapeDtypeStruct((2, RING, piece, 512), i16),
            jax.ShapeDtypeStruct((RING, piece, facts), bf16),
        ],
        in_specs=[vmem] * 3,
        out_specs=[vmem] * 6,
        scratch_shapes=[
            pltpu.VMEM((blocks, n, lanes), bf16),
            pltpu.VMEM((blocks, piece, lanes), bf16),
            pltpu.VMEM((blocks, facts, lanes), bf16),
            pltpu.VMEM((n, n), f32),
            pltpu.VMEM((128, 128), f32),
            pltpu.VMEM((128, 128), f32),
            pltpu.VMEM((piece, n), f32),
            pltpu.VMEM((n, facts), f32),
            pltpu.VMEM((piece, facts), f32),
            dma, dma, dma((UNITS,)), dma, dma((RING - 1,)), dma((RING - 1,)),
            dma((ROWS * COLS - 1,)), dma((UNITS,)), dma((UNITS,)), dma((UNITS,)),
            dma((RING - 1,)), dma((RING - 1,)), dma((RING - 1,)), dma((RING - 1,)), dma, dma,
        ],
        compiler_params=pltpu.CompilerParams(collective_id=1, has_side_effects=True, vmem_limit_bytes=52 << 20),
        name="panel_factor",
    )(keys, spots, regular)


def finish_kernel(first, g, e, factor, inv_hi, inv_lo, solved, solved_rows, res, l_out, u_out):
    n = factor.shape[1]
    parts, piece = g.shape[1:3]
    rows = parts * piece
    nt, nn = ((1,), (1,)), ((1,), (0,))

    def send(weight):
        a, b = split(weight)
        u_out[...] = dot(a, res[...], nn) + dot(b, res[...], nn)

    @pl.when(first[0] == 0)
    def _():
        l_out[...] = factor[...]
        send(solved_rows[...])

    @pl.when(first[0] != 0)
    def _():
        whole = jnp.concatenate([jnp.concatenate([g[0, i], g[1, i]], axis=1) for i in range(parts)], axis=0).astype(i32)
        scale = jnp.exp(whole[:, n:n + 1].astype(f32) * STEP) * (1.0 / TOP)
        whole = whole[:, :n]
        high = lax.shift_right_arithmetic(whole, 8)
        low = (whole - high * 256).astype(f32).astype(bf16)
        high = high.astype(f32).astype(bf16)
        for lo in range(0, n, 256):
            hi = min(lo + 256, n)
            at = slice(lo, hi)
            a, b = inv_hi[at, :hi], inv_lo[at, :hi]
            big = dot(high[:, :hi], a, nt) + dot(high[:, :hi], b, nt)
            l_out[:, at] = (big * 256.0 + dot(low[:, :hi], a, nt)) * scale
        a, b = split(l_out[...])
        c, d = split(solved[...])
        ends = jnp.concatenate([e[i] for i in range(parts)], axis=0).astype(f32)
        send(ends - (dot(a, c, nn) + dot(a, d, nn) + dot(b, c, nn)))


def finish_call(first, g, e, factor, inv_hi, inv_lo, solved, res):
    n, facts = solved.shape
    piece, width = g.shape[2:]
    parts = 2
    rows = parts * piece
    full = lambda *shape: pl.BlockSpec(shape, lambda i: (0,) * len(shape))
    return pl.pallas_call(
        finish_kernel,
        grid=(RING // parts,),
        out_shape=[jax.ShapeDtypeStruct((n, n), f32), jax.ShapeDtypeStruct((n, res.shape[1]), f32)],
        in_specs=[
            pl.BlockSpec(memory_space=pltpu.SMEM),
            pl.BlockSpec((2, parts, piece, width), lambda i: (0, i, 0, 0)),
            pl.BlockSpec((parts, piece, facts), lambda i: (i, 0, 0)),
            pl.BlockSpec((rows, n), lambda i: (i, 0)),
            full(n, n),
            full(n, n),
            full(n, facts),
            pl.BlockSpec((rows, facts), lambda i: (i, 0)),
            full(*res.shape),
        ],
        out_specs=[pl.BlockSpec((rows, n), lambda i: (i, 0)), pl.BlockSpec((rows, res.shape[1]), lambda i: (i, 0))],
        compiler_params=pltpu.CompilerParams(vmem_limit_bytes=40 << 20),
        name="panel_rows",
    )(first, g, e, factor, inv_hi, inv_lo, solved, solved, res)


def on_device(tokens_in, gate_weight, up_weight, doc_lengths, subject_raw, residuals, regular):
    docs = jnp.broadcast_to(jnp.concatenate([doc_lengths, subject_raw], axis=1).reshape(-1, 1), (16, 128))
    keys, spots = project_call(tokens_in, gate_weight, up_weight, docs)
    factor, inv_hi, inv_lo, solved, g_all, e_all = factor_call(keys, spots, regular.reshape(1, -1))
    block_index = lax.axis_index(("row", "col")).astype(i32).reshape(1)
    return tuple(finish_call(block_index, g_all, e_all, factor, inv_hi, inv_lo, solved, residuals))


def solution(mesh):
    return jax.shard_map(
        on_device,
        mesh=mesh,
        in_specs=(
            P(("row", "col"), "doc"),
            P("doc", ("row", "col")),
            P("doc", ("row", "col")),
            P("doc", None),
            P("doc", None),
            P(None, "doc"),
            P(),
        ),
        out_specs=(P(("row", "col"), None), P(("row", "col"), "doc")),
        check_vma=False,
    )
```

```python
import functools
import math

import jax
import jax.numpy as jnp
from jax import lax
from jax.experimental import pallas as pl
from jax.experimental.pallas import tpu as pltpu
from jax.sharding import PartitionSpec as P

HI = lax.Precision.HIGHEST
MESH = pl.DeviceIdType.MESH
f32, bf16, i16, i32 = jnp.float32, jnp.bfloat16, jnp.int16, jnp.int32

ROWS, COLS, RING = 4, 4, 8
UNITS = 8
LAG = 2
LN2 = math.log(2.0)
STEP = LN2 / 64
TOP = 32700.0


def dot(a, b, dims, precision=None):
    return lax.dot_general(a, b, (dims, ((), ())), precision=precision, preferred_element_type=f32)


def spread_row(v, k):
    return jnp.broadcast_to(v[k:k + 1, :], v.shape)


def spread_lane(v, j):
    return jnp.broadcast_to(v[:, j:j + 1], v.shape)


def factor_block(load, store):
    sub = lax.broadcasted_iota(jnp.int32, (8, 128), 0)
    lane = lax.broadcasted_iota(jnp.int32, (8, 128), 1)
    left = [load(i) for i in range(16)]
    right = [jnp.where(lane == sub + 8 * i, 1.0, 0.0).astype(f32) for i in range(16)]
    for p in range(16):
        cols = [spread_lane(left[p], 8 * p + k) for k in range(8)]
        below = {i: [spread_lane(left[i], 8 * p + k) for k in range(8)] for i in range(p + 1, 16)}
        pivots = jnp.zeros((8, 128), f32)
        a, v = left[p], right[p]
        for k in range(8):
            pivot = spread_row(cols[k], k)
            inv = 1.0 / pivot
            pivots = jnp.where(sub == k, pivot, pivots)
            ak, vk = spread_row(a, k), spread_row(v, k)
            lead = {m: spread_row(cols[m], k) for m in range(k + 1, 8)}
            mult = jnp.where(sub > k, cols[k] * inv, 0.0)
            for m in range(k + 1, 8):
                cols[m] = cols[m] - mult * lead[m]
            a = a - mult * ak
            v = v - mult * vk
            for i in range(p + 1, 16):
                part = below[i][k] * inv
                for m in range(k + 1, 8):
                    below[i][m] = below[i][m] - part * lead[m]
                left[i] = left[i] - part * ak
                right[i] = right[i] - part * vk
        scale = lax.rsqrt(pivots)
        store(p, jnp.where(lane >= sub + 8 * p, a * scale, 0.0), v * scale)


def place():
    doc = lax.axis_index("doc")
    return doc // 2, lax.rem(doc, 2), lax.axis_index("row"), lax.axis_index("col")


def at_device(z, core, row, col):
    return {"doc": z * 2 + core, "row": row, "col": col}


def greet(z, core, row, col, ring_steps):
    barrier = pltpu.get_barrier_semaphore()
    count = 0
    for dr in range(ROWS):
        for dc in range(COLS):
            for other in range(2):
                if dr == 0 and dc == 0 and other == 0:
                    continue
                device = at_device(z, lax.rem(core + other, 2), lax.rem(row + dr, ROWS), lax.rem(col + dc, COLS))
                pl.semaphore_signal(barrier, inc=1, device_id=device, device_id_type=MESH)
                count += 1
    for step in ring_steps:
        pl.semaphore_signal(barrier, inc=1, device_id=at_device(lax.rem(z + step, RING), core, row, col), device_id_type=MESH)
        count += 1
    return barrier, count


def remote(src, dst, send, recv, device):
    return pltpu.make_async_remote_copy(
        src_ref=src, dst_ref=dst, send_sem=send, recv_sem=recv, device_id=device, device_id_type=MESH
    )


def tile(start, size):
    return pl.ds(pl.multiple_of(start, size), size)


def whole_kernel(tok_ref, wg_ref, wu_ref, docs, regular, res, l_out, u_out,
                 tok, wg, wu, spots, xg, wt, part, far_out, far_in, near_out, near_in,
                 k0, kb, select, m, up, inv, grams, edit0, edit, g_all, e_all, inv_hi, inv_lo,
                 ls, qs, qr, os, orr, t1, t2, t3, xr, ws, wr, fs, fr, ns, nr,
                 ps, pr, ss, sr, zs, zr, b1, b2, b3, br, hs, hr, gs, gr, es, er, vs, vr):
    z, core, row, col = place()
    loads = [pltpu.make_async_copy(a, b, ls.at[i]) for i, (a, b) in enumerate(((tok_ref, tok), (wg_ref, wg), (wu_ref, wu)))]
    for load in loads:
        load.start()
    depth, width = wg.shape
    piece = width // RING
    lanes = tok.shape[0]
    odd = lax.rem(row, 2)
    first = odd * COLS + col
    mine = row // 2
    holder = core == mine
    origin = jnp.logical_and(row == 0, col == 0)

    def rows_of(zz):
        return pl.ds(pl.multiple_of(zz * piece, 16), piece)

    def in_row(step):
        return at_device(z, core, row, lax.rem(col + step, COLS))

    def in_column(step):
        return at_device(z, core, lax.rem(row + step, ROWS), col)

    barrier, count = greet(z, core, row, col, tuple(range(1, RING)))
    sub = lax.broadcasted_iota(i32, (8, 128), 0)
    lengths = docs[:8, :].astype(f32)
    raw = docs[8:, :].astype(f32)
    starts = jnp.zeros((8, 128), f32)
    for j in range(7):
        starts = starts + jnp.where(sub > j, jnp.broadcast_to(lengths[j:j + 1, :], (8, 128)), 0.0)
    wrapped = raw - lengths * jnp.floor((raw + 0.5) / lengths)
    spots[core, z] = starts + wrapped + ((z * 2 + core) * lanes).astype(f32)
    pl.semaphore_wait(barrier, count)

    def spot_copy(dz):
        here = spots.at[core, z]
        return remote(here, here, qs.at[dz - 1], qr.at[dz - 1], at_device(lax.rem(z + dz, RING), core, row, col))

    loads[0].wait()

    def token_first(step):
        slot = xg.at[first, core]
        x_way = at_device(z, mine, lax.rem(row + step * (1 - core), ROWS), lax.rem(col + step * core, COLS))
        return remote(tok, slot, t1.at[step], xr.at[first, core], x_way)

    for step in (0, 3, 2, 1):
        if step:
            token_first(step).start()
        else:
            @pl.when(core != mine)
            def _():
                token_first(0).start()

    @pl.when(holder)
    def _():
        xg[first, core] = tok[...]

    partner = at_device(z, 1 - core, row, col)

    def weight_copy(j):
        rows = tile(j * 128, 128)
        return remote(wt.at[core, rows], wt.at[core, rows], ws.at[j], wr.at[j], partner)

    tiles = width // 128
    loads[1].wait()
    loads[2].wait()

    def turn(j, _):
        at = tile(j * 128, 128)
        wt[core, at, :] = wg[:, at].T
        weight_copy(j).start()
        wt[core, tile((j + tiles) * 128, 128), :] = wu[:, at].T
        weight_copy(j + tiles).start()
        return 0

    def here_tokens(t, half):
        slot = xg.at[t, half]
        remote(slot, slot, t1.at[0], xr.at[t, half], partner).wait_recv()

    def token_row(s, step):
        slot = xg.at[s * COLS + col, 0]
        return remote(slot, slot, t2.at[s, step - 1], xr.at[s * COLS + col, 0], in_row(step))

    def token_column(j, step):
        t = odd * COLS + lax.rem(col + j, COLS)
        return remote(xg.at[t, 1], xg.at[t, 1], t3.at[j, step - 1], xr.at[t, 1], in_column(step))

    lax.fori_loop(0, 3, turn, 0)
    for s in range(2):
        @pl.when(jnp.logical_not(jnp.logical_and(holder, jnp.logical_and(core == 0, odd == s))))
        def _(s=s):
            here_tokens(s * COLS + col, 0)
        for step in (3, 2, 1):
            token_row(s, step).start()

    @pl.when(holder)
    def _():
        for j in range(COLS):
            if j == 0:
                @pl.when(core == 0)
                def _():
                    here_tokens(first, 1)
            else:
                here_tokens(odd * COLS + lax.rem(col + j, COLS), 1)
            for step in (1, 3, 2):
                token_column(j, step).start()

    lax.fori_loop(3, tiles, turn, 0)
    for dz in range(1, RING):
        spot_copy(dz).start()

    def spot_of(u):
        return lax.rem(u, 2) * COLS + lax.rem(col + u // 2, COLS)

    def settled(t, half):
        if half == 0:
            return lax.rem(t, COLS) == col
        return jnp.logical_and(holder, t // COLS == odd)

    def wait_tokens(u):
        for half in range(2):
            @pl.when(jnp.logical_not(settled(spot_of(u), half)))
            def _(half=half):
                here_tokens(spot_of(u), half)

    def project(pair):
        wait_tokens(2 * pair)
        wait_tokens(2 * pair + 1)
        x = [jnp.concatenate([xg[spot_of(2 * pair), half], xg[spot_of(2 * pair + 1), half]], axis=0) for half in range(2)]

        def chunk(j, _):
            rows = tile(j * 448, 448)
            total = dot(wt[0, rows, :], x[0], ((1,), (1,))) + dot(wt[1, rows, :], x[1], ((1,), (1,)))
            part[2 * pair, rows, :] = total[:, :lanes]
            part[2 * pair + 1, rows, :] = total[:, lanes:]
            return 0

        lax.fori_loop(0, 2 * width // 448, chunk, 0)

    def own(u, target):
        return (
            part[u, pl.ds(pl.multiple_of(target * piece, 16), piece), :],
            part[u, pl.ds(pl.multiple_of(width + target * piece, 16), piece), :],
        )

    def opened(slot):
        scale = jnp.exp(slot[2 * piece:, :].astype(i32).astype(f32)[:1] * STEP) * (1.0 / TOP)
        return (
            slot[:piece, :].astype(i32).astype(f32) * scale,
            slot[piece:2 * piece, :].astype(i32).astype(f32) * scale,
        )

    def packed(slot, g, v):
        top = jnp.maximum(jnp.max(jnp.abs(g), axis=0, keepdims=True), jnp.max(jnp.abs(v), axis=0, keepdims=True))
        grade = jnp.ceil(jnp.log(jnp.maximum(top, 1e-30)) * (1.0 / STEP)) + 1.0
        up = jnp.exp(grade * -STEP) * TOP
        slot[:piece, :] = jnp.round(g * up).astype(i32).astype(i16)
        slot[piece:2 * piece, :] = jnp.round(v * up).astype(i32).astype(i16)
        slot[2 * piece:, :] = jnp.broadcast_to(grade.astype(i32), (16, lanes)).astype(i16)

    def sign(u):
        return 1 - 2 * lax.rem(u, 2)

    def far(u, hop):
        return remote(far_out.at[u, hop], far_in.at[u, hop], fs.at[u, hop], fr.at[u, hop],
                      at_device(lax.rem(z + sign(u) + RING, RING), core, row, col))

    def near(u, hop):
        return remote(near_out.at[u, hop], near_in.at[u, hop], ns.at[u, hop], nr.at[u, hop],
                      at_device(lax.rem(z - sign(u) + RING, RING), core, row, col))

    def pass_on(u, hop):
        g, v = own(u, lax.rem(z + sign(u) * (4 - hop) + RING, RING))
        if hop:
            far(u, hop - 1).wait_recv()
            a, b = opened(far_in.at[u, hop - 1])
            g, v = g + a, v + b
        packed(far_out.at[u, hop], g, v)
        far(u, hop).start()
        if hop < 3:
            g, v = own(u, lax.rem(z - sign(u) * (3 - hop) + RING, RING))
            if hop:
                near(u, hop - 1).wait_recv()
                a, b = opened(near_in.at[u, hop - 1])
                g, v = g + a, v + b
            packed(near_out.at[u, hop], g, v)
            near(u, hop).start()

    def scatter(t):
        return remote(kb.at[core * UNITS + t], k0.at[core * UNITS + t, rows_of(z)], ss.at[t], sr,
                      at_device(z, core, 2 * core + t // COLS, lax.rem(t, COLS)))

    def finish(u):
        g, v = own(u, z)
        near(u, 2).wait_recv()
        a, b = opened(near_in.at[u, 2])
        g, v = g + a, v + b
        far(u, 3).wait_recv()
        a, b = opened(far_in.at[u, 3])
        g, v = g + a, v + b
        t = spot_of(u)
        kb[core * UNITS + t] = (g * (1.0 / (1.0 + jnp.exp(-g))) * v).astype(bf16)
        home = jnp.logical_and(core == 0, t == 0)

        @pl.when(jnp.logical_and(origin, home))
        def _():
            k0[0, rows_of(z), :] = kb[0]

        @pl.when(jnp.logical_and(origin, jnp.logical_not(home)))
        def _():
            scatter(t).start()

    def weights_here(j, _):
        rows = tile(j * 128, 128)
        remote(wt.at[1 - core, rows], wt.at[1 - core, rows], ws.at[j], wr.at[j], partner).wait_recv()
        return 0

    lax.fori_loop(0, 2 * tiles, weights_here, 0)

    def step(g, _):
        for hop in range(1, 5):
            @pl.when(jnp.logical_and(g >= LAG * hop, g < UNITS + LAG * hop))
            def _(hop=hop):
                if hop < 4:
                    pass_on(g - LAG * hop, hop)
                else:
                    finish(g - LAG * hop)

        @pl.when(jnp.logical_and(lax.rem(g, 2) == 0, g < UNITS))
        def _():
            project(g // 2)

        @pl.when(g < UNITS)
        def _():
            pass_on(g, 0)

        return 0

    lax.fori_loop(0, UNITS + 4 * LAG, step, 0)

    own_keys = kb.at[pl.ds(core * UNITS, UNITS)]
    pair = remote(own_keys, own_keys, ps, pr, partner)
    pair.start()
    n, tokens = k0.shape[1], 2 * UNITS * lanes
    half_rows = n // 2

    def along(dz):
        here = k0.at[core * UNITS + first, rows_of(z)]
        return remote(here, here, zs.at[dz - 1], zr.at[dz - 1], at_device(lax.rem(z + dz, RING), core, row, col))

    def half_of(t, half):
        return k0.at[core * UNITS + t, pl.ds(half * half_rows, half_rows)]

    def block_first(half, step):
        here = half_of(first, half)
        return remote(here, here, b1.at[half, step - 1], br.at[first, half], in_row(step) if half else in_column(step))

    def block_row(s, step):
        t = s * COLS + col
        return remote(half_of(t, 0), half_of(t, 0), b2.at[s, step - 1], br.at[t, 0], in_row(step))

    def block_column(j, step):
        t = odd * COLS + lax.rem(col + j, COLS)
        return remote(half_of(t, 1), half_of(t, 1), b3.at[j, step - 1], br.at[t, 1], in_column(step))

    def here_block(t, half):
        remote(half_of(t, half), half_of(t, half), b1.at[0, 0], br.at[t, half], partner).wait_recv()

    @pl.when(holder)
    def _():
        @pl.when(jnp.logical_not(jnp.logical_and(origin, core == 0)))
        def _():
            here = k0.at[core * UNITS + first, rows_of(z)]
            remote(here, here, ss.at[0], sr, partner).wait_recv()

        for dz in range(1, RING):
            along(dz).start()

    for dz in range(1, RING):
        there = spots.at[core, lax.rem(z - dz + RING, RING)]
        remote(there, there, qs.at[dz - 1], qr.at[dz - 1], partner).wait_recv()
    over = remote(spots.at[core], spots.at[core], os, orr, partner)
    over.start()
    remote(spots.at[1 - core], spots.at[1 - core], os, orr, partner).wait_recv()
    over.wait_send()
    for dz in range(1, RING):
        spot_copy(dz).wait_send()

    lane = lax.broadcasted_iota(i32, (128, 128), 1)
    spots_row = jnp.concatenate([spots[group % 2, group // 2] for group in range(2 * RING)], axis=0).astype(i32)
    for b in range(2 * UNITS):
        select[b] = jnp.where(lane + b * lanes == spots_row, 1.0, 0.0).astype(bf16)
    m[...] = jnp.zeros((n, n), f32)
    grams[...] = jnp.zeros(grams.shape, f32)
    edit0[...] = jnp.zeros(edit0.shape, f32)
    edit[...] = jnp.zeros(edit.shape, f32)

    @pl.when(holder)
    def _():
        for dz in range(1, RING):
            there = k0.at[core * UNITS + first, rows_of(lax.rem(z - dz + RING, RING))]
            remote(there, there, zs.at[dz - 1], zr.at[dz - 1], partner).wait_recv()
        for step in (3, 1, 2):
            for half in range(2):
                block_first(half, step).start()

    for s in range(2):
        @pl.when(jnp.logical_not(jnp.logical_and(holder, odd == s)))
        def _(s=s):
            here_block(s * COLS + col, 0)
        for step in (3, 2, 1):
            block_row(s, step).start()

    @pl.when(holder)
    def _():
        for j in range(COLS):
            if j:
                here_block(odd * COLS + lax.rem(col + j, COLS), 1)
            for step in (1, 3, 2):
                block_column(j, step).start()

    mid = n // 256 * 128 + 128
    nt = ((1,), (1,))

    def hand_over(c, t):
        here = k0.at[c * UNITS + t]
        return remote(here, here, hs.at[t], hr.at[t], partner)

    def add_pair(c, q):
        b0, b1_ = c * UNITS + spot_of(2 * q), c * UNITS + spot_of(2 * q + 1)
        a = jnp.concatenate([k0[b0], k0[b1_]], axis=1)
        own = jnp.concatenate([kb[b0], kb[b1_]], axis=1)
        hot = jnp.concatenate([select[b0], select[b1_]], axis=1)
        m[:mid, :] = m[:mid, :] + dot(a[:mid], a, nt)
        m[mid:, mid:] = m[mid:, mid:] + dot(a[mid:], a[mid:], nt)
        grams[...] = grams[...] + dot(own, a, nt)
        edit0[...] = edit0[...] + dot(a, hot, nt)
        edit[...] = edit[...] + dot(own, hot, nt)

    their_keys = kb.at[pl.ds((1 - core) * UNITS, UNITS)]
    remote(their_keys, their_keys, ps, pr, partner).wait_recv()

    def near_pair(q, _):
        for j in range(2):
            t = spot_of(2 * q + j)
            for half in range(2):
                @pl.when(jnp.logical_not(settled(t, half)))
                def _(t=t, half=half):
                    here_block(t, half)
            hand_over(core, t).start()
        add_pair(core, q)
        return 0

    lax.fori_loop(0, UNITS // 2, near_pair, 0)

    def far_pair(q, _):
        for j in range(2):
            hand_over(1 - core, spot_of(2 * q + j)).wait_recv()
        add_pair(1 - core, q)
        return 0

    lax.fori_loop(0, UNITS // 2, far_pair, 0)

    share = 1.0 / tokens
    top = jnp.max(jnp.abs(grams[...]), axis=1, keepdims=True) * share
    grade = jnp.ceil(jnp.log(jnp.maximum(top, 1e-30)) * (1.0 / STEP)) + 1.0
    scaled = jnp.round(grams[...] * (jnp.exp(grade * -STEP) * (TOP * share))).astype(i32).astype(i16)
    half = g_all.shape[3]

    @pl.when(core == 0)
    def _():
        g_all[0, z] = scaled[:, :half]

    @pl.when(core == 1)
    def _():
        g_all[1, z, :, :n - half] = scaled[:, half:]
        g_all[1, z, :, n - half:] = jnp.broadcast_to(grade.astype(i32), (piece, 2 * half - n)).astype(i16)

    e_all[z] = edit[...].astype(bf16)

    def give(dz):
        there = at_device(lax.rem(z + dz, RING), core, row, col)
        g, e = g_all.at[core, z], e_all.at[z]
        return (remote(g, g, gs.at[dz - 1], gr.at[dz - 1], there), remote(e, e, es.at[dz - 1], er.at[dz - 1], there))

    def take(dz):
        source = lax.rem(z - dz + RING, RING)
        g, e = g_all.at[core, source], e_all.at[source]
        return (remote(g, g, gs.at[dz - 1], gr.at[dz - 1], partner), remote(e, e, es.at[dz - 1], er.at[dz - 1], partner))

    for dz in range(1, RING):
        for copy in give(dz):
            copy.start()
    give_over = remote(g_all.at[core], g_all.at[core], vs, vr, partner)

    blocks = n // 128
    r_i = lax.broadcasted_iota(i32, (128, 128), 0)
    c_i = lax.broadcasted_iota(i32, (128, 128), 1)
    m[...] = m[...] * share
    for k in range(blocks):
        at = slice(k * 128, (k + 1) * 128)
        m[at, at] = m[at, at] + jnp.where(r_i == c_i, jnp.broadcast_to(regular[:, at], (128, 128)), 0.0)
    l_out[...] = jnp.zeros((n, n), f32)

    def step(k, _):
        at = pl.ds(pl.multiple_of(k * 128, 128), 128)

        def load(i):
            return m[pl.ds(pl.multiple_of(k * 128 + 8 * i, 8), 8), at]

        def store(i, a, v):
            up[8 * i:8 * i + 8, :] = a
            inv[8 * i:8 * i + 8, :] = v

        factor_block(load, store)
        l_out[at, at] = up[...].T

        @pl.when(k == blocks - 2)
        def _():
            for dz in range(1, RING):
                for copy in take(dz):
                    copy.wait_recv()
            give_over.start()

        for fixed in range(blocks):
            @pl.when(k == fixed)
            def _(fixed=fixed):
                lo, hi = fixed * 128, (fixed + 1) * 128
                li = inv[...]
                if fixed:
                    m[lo:hi, :lo] = dot(li, m[lo:hi, :lo], ((1,), (0,)), HI)
                m[lo:hi, lo:hi] = li
                if hi < n:
                    m[lo:hi, hi:] = dot(li, m[lo:hi, hi:], ((1,), (0,)), HI)
                    lt = m[lo:hi, hi:].T
                    l_out[hi:, lo:hi] = lt
                    for rlo in range(hi, n, 128):
                        rows = slice(rlo, rlo + 128)
                        cut = lt[rlo - hi:rlo - hi + 128]
                        if fixed:
                            m[rows, :lo] = m[rows, :lo] - dot(cut, m[lo:hi, :lo], ((1,), (0,)), HI)
                        m[rows, lo:hi] = -dot(cut, li, ((1,), (0,)), HI)
                        m[rows, rlo:] = m[rows, rlo:] - dot(cut, m[lo:hi, rlo:], ((1,), (0,)), HI)
        return 0

    lax.fori_loop(0, blocks, step, 0)
    for k in range(blocks - 1):
        lo, hi = k * 128, (k + 1) * 128
        m[lo:hi, hi:] = jnp.zeros((128, n - hi), f32)
    solved = dot(m[...], edit0[...], ((1,), (0,)), HI)
    edit0[...] = solved
    whole, rest = split(m[...])
    inv_hi[...] = whole
    inv_lo[...] = rest
    remote(g_all.at[1 - core], g_all.at[1 - core], vs, vr, partner).wait_recv()
    nn = ((1,), (0,))

    def send(rows, weight):
        a, b = split(weight)
        u_out[rows, :] = dot(a, res[...], nn) + dot(b, res[...], nn)

    @pl.when(origin)
    def _():
        send(pl.ds(0, n), edit0[...])

    @pl.when(jnp.logical_not(origin))
    def _():
        c, d = split(edit0[...])

        def rows_part(i, _):
            rows = tile(i * 2 * piece, 2 * piece)
            g = jnp.concatenate([
                jnp.concatenate([g_all[0, 2 * i + s], g_all[1, 2 * i + s]], axis=1) for s in range(2)
            ], axis=0).astype(i32)
            scale = jnp.exp(g[:, n:n + 1].astype(f32) * STEP) * (1.0 / TOP)
            g = g[:, :n]
            high = lax.shift_right_arithmetic(g, 8)
            low = (g - high * 256).astype(f32).astype(bf16)
            high = high.astype(f32).astype(bf16)
            for lo in range(0, n, 256):
                hi = min(lo + 256, n)
                at = slice(lo, hi)
                a, b = inv_hi[at, :hi], inv_lo[at, :hi]
                big = dot(high[:, :hi], a, nt) + dot(high[:, :hi], b, nt)
                l_out[rows, at] = (big * 256.0 + dot(low[:, :hi], a, nt)) * scale
            a, b = split(l_out[rows, :])
            ends = jnp.concatenate([e_all[2 * i], e_all[2 * i + 1]], axis=0).astype(f32)
            send(rows, ends - (dot(a, c, nn) + dot(a, d, nn) + dot(b, c, nn)))
            return 0

        lax.fori_loop(0, RING // 2, rows_part, 0)

    give_over.wait_send()
    for dz in range(1, RING):
        for copy in give(dz):
            copy.wait_send()
    pair.wait_send()
    for t in range(UNITS):
        hand_over(core, t).wait_send()

    @pl.when(origin)
    def _():
        for t in range(UNITS):
            if t == 0:
                @pl.when(core == 1)
                def _():
                    scatter(0).wait_send()
            else:
                scatter(t).wait_send()

    for step in (1, 2, 3):
        token_first(step).wait_send()
        for s in range(2):
            token_row(s, step).wait_send()
            block_row(s, step).wait_send()

    @pl.when(core != mine)
    def _():
        token_first(0).wait_send()

    @pl.when(holder)
    def _():
        for dz in range(1, RING):
            along(dz).wait_send()
        for step in (1, 2, 3):
            for half in range(2):
                block_first(half, step).wait_send()
            for j in range(COLS):
                token_column(j, step).wait_send()
                block_column(j, step).wait_send()

    def sent(j, _):
        weight_copy(j).wait_send()
        return 0

    lax.fori_loop(0, 2 * tiles, sent, 0)

    def ring_sent(u, _):
        for hop in range(4):
            far(u, hop).wait_send()
            if hop < 3:
                near(u, hop).wait_send()
        return 0

    lax.fori_loop(0, UNITS, ring_sent, 0)


def split(a):
    whole = a.astype(bf16)
    return whole, (a - whole.astype(f32)).astype(bf16)


def whole_call(tok, wg, wu, docs, regular, res):
    lanes, depth = tok.shape
    width = wg.shape[1]
    piece = width // RING
    rows = 2 * piece + 16
    n, blocks, facts = width, 2 * UNITS, 8 * 2 * RING
    dma = pltpu.SemaphoreType.DMA
    vmem = pl.BlockSpec(memory_space=pltpu.VMEM)
    tiles = 2 * width // 128
    return pl.pallas_call(
        whole_kernel,
        out_shape=[jax.ShapeDtypeStruct((n, n), f32), jax.ShapeDtypeStruct((n, res.shape[1]), f32)],
        in_specs=[pl.BlockSpec(memory_space=pl.ANY)] * 3 + [vmem] * 3,
        out_specs=[vmem] * 2,
        scratch_shapes=[
            pltpu.VMEM((lanes, depth), bf16),
            pltpu.VMEM((depth, width), bf16),
            pltpu.VMEM((depth, width), bf16),
            pltpu.VMEM((2, RING, 8, 128), f32),
            pltpu.VMEM((UNITS, 2, lanes, depth), bf16),
            pltpu.VMEM((2, 2 * width, depth), bf16),
            pltpu.VMEM((UNITS, 2 * width, lanes), f32),
            pltpu.VMEM((UNITS, 4, rows, lanes), i16),
            pltpu.VMEM((UNITS, 4, rows, lanes), i16),
            pltpu.VMEM((UNITS, 3, rows, lanes), i16),
            pltpu.VMEM((UNITS, 3, rows, lanes), i16),
            pltpu.VMEM((blocks, n, lanes), bf16),
            pltpu.VMEM((blocks, piece, lanes), bf16),
            pltpu.VMEM((blocks, facts, lanes), bf16),
            pltpu.VMEM((n, n), f32),
            pltpu.VMEM((128, 128), f32),
            pltpu.VMEM((128, 128), f32),
            pltpu.VMEM((piece, n), f32),
            pltpu.VMEM((n, facts), f32),
            pltpu.VMEM((piece, facts), f32),
            pltpu.VMEM((2, RING, piece, 512), i16),
            pltpu.VMEM((RING, piece, facts), bf16),
            pltpu.VMEM((n, n), bf16),
            pltpu.VMEM((n, n), bf16),
            dma((3,)), dma((RING - 1,)), dma((RING - 1,)), dma, dma,
            dma((4,)), dma((2, 3)), dma((COLS, 3)), dma((UNITS, 2)), dma((tiles,)), dma((tiles,)),
            dma((UNITS, 4)), dma((UNITS, 4)), dma((UNITS, 3)), dma((UNITS, 3)),
            dma, dma, dma((UNITS,)), dma, dma((RING - 1,)), dma((RING - 1,)),
            dma((2, 3)), dma((2, 3)), dma((COLS, 3)), dma((UNITS, 2)), dma((UNITS,)), dma((UNITS,)),
            dma((RING - 1,)), dma((RING - 1,)), dma((RING - 1,)), dma((RING - 1,)), dma, dma,
        ],
        compiler_params=pltpu.CompilerParams(collective_id=0, has_side_effects=True, vmem_limit_bytes=60 << 20),
        name="panel_edit",
    )(tok, wg, wu, docs, regular, res)


def on_device(tokens_in, gate_weight, up_weight, doc_lengths, subject_raw, residuals, regular):
    docs = jnp.broadcast_to(jnp.concatenate([doc_lengths, subject_raw], axis=1).reshape(-1, 1), (16, 128))
    return tuple(whole_call(tokens_in, gate_weight, up_weight, docs, regular.reshape(1, -1), residuals))


def solution(mesh):
    return jax.shard_map(
        on_device,
        mesh=mesh,
        in_specs=(
            P(("row", "col"), "doc"),
            P("doc", ("row", "col")),
            P("doc", ("row", "col")),
            P("doc", None),
            P("doc", None),
            P(None, "doc"),
            P(),
        ),
        out_specs=(P(("row", "col"), None), P(("row", "col"), "doc")),
        check_vma=False,
    )
```

```python
import functools
import math

import jax
import jax.numpy as jnp
from jax import lax
from jax.experimental import pallas as pl
from jax.experimental.pallas import tpu as pltpu
from jax.sharding import PartitionSpec as P

HI = lax.Precision.HIGHEST
MESH = pl.DeviceIdType.MESH
f32, bf16, i16, i32 = jnp.float32, jnp.bfloat16, jnp.int16, jnp.int32

ROWS, COLS, RING = 4, 4, 8
UNITS = 8
LAG = 3
LN2 = math.log(2.0)
STEP = LN2 / 64
TOP = 32700.0


def dot(a, b, dims, precision=None):
    return lax.dot_general(a, b, (dims, ((), ())), precision=precision, preferred_element_type=f32)


def spread_row(v, k):
    return jnp.broadcast_to(v[k:k + 1, :], v.shape)


def spread_lane(v, j):
    return jnp.broadcast_to(v[:, j:j + 1], v.shape)


def factor_block(load, store):
    sub = lax.broadcasted_iota(jnp.int32, (8, 128), 0)
    lane = lax.broadcasted_iota(jnp.int32, (8, 128), 1)
    left = [load(i) for i in range(16)]
    right = [jnp.where(lane == sub + 8 * i, 1.0, 0.0).astype(f32) for i in range(16)]
    for p in range(16):
        cols = [spread_lane(left[p], 8 * p + k) for k in range(8)]
        below = {i: [spread_lane(left[i], 8 * p + k) for k in range(8)] for i in range(p + 1, 16)}
        pivots = jnp.zeros((8, 128), f32)
        a, v = left[p], right[p]
        for k in range(8):
            pivot = spread_row(cols[k], k)
            inv = 1.0 / pivot
            pivots = jnp.where(sub == k, pivot, pivots)
            ak, vk = spread_row(a, k), spread_row(v, k)
            lead = {m: spread_row(cols[m], k) for m in range(k + 1, 8)}
            mult = jnp.where(sub > k, cols[k] * inv, 0.0)
            for m in range(k + 1, 8):
                cols[m] = cols[m] - mult * lead[m]
            a = a - mult * ak
            v = v - mult * vk
            for i in range(p + 1, 16):
                part = below[i][k] * inv
                for m in range(k + 1, 8):
                    below[i][m] = below[i][m] - part * lead[m]
                left[i] = left[i] - part * ak
                right[i] = right[i] - part * vk
        scale = lax.rsqrt(pivots)
        store(p, jnp.where(lane >= sub + 8 * p, a * scale, 0.0), v * scale)


def place():
    doc = lax.axis_index("doc")
    return doc // 2, lax.rem(doc, 2), lax.axis_index("row"), lax.axis_index("col")


def at_device(z, core, row, col):
    return {"doc": z * 2 + core, "row": row, "col": col}


def greet(z, core, row, col, ring_steps):
    barrier = pltpu.get_barrier_semaphore()
    count = 0
    for dr in range(ROWS):
        for dc in range(COLS):
            for other in range(2):
                if dr == 0 and dc == 0 and other == 0:
                    continue
                device = at_device(z, lax.rem(core + other, 2), lax.rem(row + dr, ROWS), lax.rem(col + dc, COLS))
                pl.semaphore_signal(barrier, inc=1, device_id=device, device_id_type=MESH)
                count += 1
    for step in ring_steps:
        pl.semaphore_signal(barrier, inc=1, device_id=at_device(lax.rem(z + step, RING), core, row, col), device_id_type=MESH)
        count += 1
    return barrier, count


def remote(src, dst, send, recv, device):
    return pltpu.make_async_remote_copy(
        src_ref=src, dst_ref=dst, send_sem=send, recv_sem=recv, device_id=device, device_id_type=MESH
    )


def tile(start, size):
    return pl.ds(pl.multiple_of(start, size), size)


def whole_kernel(tok_ref, wg_ref, wu_ref, lengths_ref, raw_ref, regular, res, l_out, u_out,
                 tok, wg, wu, spots, xg, wt, part, far_out, far_in, near_out, near_in,
                 k0, kb, select, m, up, inv, grams, edit0, edit, g_all, e_all, inv_hi, inv_lo,
                 ls, qs, qr, os, orr, t1, t2, t3, xr, ws, wr, fs, fr, ns, nr,
                 ps, pr, ss, sr, zs, zr, b1, b2, b3, br, c1, c2, cr, hs, hr, gs, gr, es, er, vs, vr):
    z, core, row, col = place()
    loads = [pltpu.make_async_copy(a, b, ls.at[i]) for i, (a, b) in enumerate(((tok_ref, tok), (wg_ref, wg), (wu_ref, wu)))]
    for load in loads:
        load.start()
    depth, width = wg.shape
    piece = width // RING
    lanes = tok.shape[0]
    odd = lax.rem(row, 2)
    first = odd * COLS + col
    mine = row // 2
    holder = core == mine
    origin = jnp.logical_and(row == 0, col == 0)

    def rows_of(zz):
        return pl.ds(pl.multiple_of(zz * piece, 16), piece)

    def in_row(step):
        return at_device(z, core, row, lax.rem(col + step, COLS))

    def in_column(step):
        return at_device(z, core, lax.rem(row + step, ROWS), col)

    barrier, count = greet(z, core, row, col, tuple(range(1, RING)))
    sub = lax.broadcasted_iota(i32, (8, 128), 0)
    square = lax.broadcasted_iota(i32, (8, 8), 0) == lax.broadcasted_iota(i32, (8, 8), 1)

    def upright(ref):
        values = jnp.broadcast_to(ref[...].astype(f32), (8, 8))
        return jnp.broadcast_to(jnp.sum(jnp.where(square, values, 0.0), axis=1, keepdims=True), (8, 128))

    lengths, raw = upright(lengths_ref), upright(raw_ref)
    starts = jnp.zeros((8, 128), f32)
    for j in range(7):
        starts = starts + jnp.where(sub > j, jnp.broadcast_to(lengths[j:j + 1, :], (8, 128)), 0.0)
    wrapped = raw - lengths * jnp.floor((raw + 0.5) / lengths)
    spots[core, z] = starts + wrapped + ((z * 2 + core) * lanes).astype(f32)
    pl.semaphore_wait(barrier, count)

    def spot_copy(dz):
        here = spots.at[core, z]
        return remote(here, here, qs.at[dz - 1], qr.at[dz - 1], at_device(lax.rem(z + dz, RING), core, row, col))

    loads[0].wait()

    def token_first(step):
        slot = xg.at[first, core]
        x_way = at_device(z, mine, lax.rem(row + step * (1 - core), ROWS), lax.rem(col + step * core, COLS))
        return remote(tok, slot, t1.at[step], xr.at[first, core], x_way)

    for step in (0, 3, 2, 1):
        if step:
            token_first(step).start()
        else:
            @pl.when(core != mine)
            def _():
                token_first(0).start()

    @pl.when(holder)
    def _():
        xg[first, core] = tok[...]

    partner = at_device(z, 1 - core, row, col)

    def weight_copy(j):
        rows = tile(j * 128, 128)
        return remote(wt.at[core, rows], wt.at[core, rows], ws.at[j], wr.at[j], partner)

    tiles = width // 128
    loads[1].wait()
    loads[2].wait()

    def turn(j, _):
        at = tile(j * 128, 128)
        wt[core, at, :] = wg[:, at].T
        weight_copy(j).start()
        wt[core, tile((j + tiles) * 128, 128), :] = wu[:, at].T
        weight_copy(j + tiles).start()
        return 0

    def here_tokens(t, half):
        slot = xg.at[t, half]
        remote(slot, slot, t1.at[0], xr.at[t, half], partner).wait_recv()

    def token_row(s, step):
        slot = xg.at[s * COLS + col, 0]
        return remote(slot, slot, t2.at[s, step - 1], xr.at[s * COLS + col, 0], in_row(step))

    def token_column(j, step):
        t = odd * COLS + lax.rem(col + j, COLS)
        return remote(xg.at[t, 1], xg.at[t, 1], t3.at[j, step - 1], xr.at[t, 1], in_column(step))

    lax.fori_loop(0, 3, turn, 0)
    for s in range(2):
        @pl.when(jnp.logical_not(jnp.logical_and(holder, jnp.logical_and(core == 0, odd == s))))
        def _(s=s):
            here_tokens(s * COLS + col, 0)
        for step in (3, 2, 1):
            token_row(s, step).start()

    @pl.when(holder)
    def _():
        for j in range(COLS):
            if j == 0:
                @pl.when(core == 0)
                def _():
                    here_tokens(first, 1)
            else:
                here_tokens(odd * COLS + lax.rem(col + j, COLS), 1)
            for step in (1, 3, 2):
                token_column(j, step).start()

    lax.fori_loop(3, tiles, turn, 0)
    for dz in range(1, RING):
        spot_copy(dz).start()

    def spot_of(u):
        return lax.rem(u, 2) * COLS + lax.rem(col + u // 2, COLS)

    def settled(t, half):
        if half == 0:
            return lax.rem(t, COLS) == col
        return jnp.logical_and(holder, t // COLS == odd)

    def wait_tokens(u):
        for half in range(2):
            @pl.when(jnp.logical_not(settled(spot_of(u), half)))
            def _(half=half):
                here_tokens(spot_of(u), half)

    def project(pair):
        wait_tokens(2 * pair)
        wait_tokens(2 * pair + 1)
        x = [jnp.concatenate([xg[spot_of(2 * pair), half], xg[spot_of(2 * pair + 1), half]], axis=0) for half in range(2)]

        def chunk(j, _):
            rows = tile(j * 448, 448)
            total = dot(wt[0, rows, :], x[0], ((1,), (1,))) + dot(wt[1, rows, :], x[1], ((1,), (1,)))
            part[2 * pair, rows, :] = total[:, :lanes]
            part[2 * pair + 1, rows, :] = total[:, lanes:]
            return 0

        lax.fori_loop(0, 2 * width // 448, chunk, 0)

    def own(u, target):
        return (
            part[u, pl.ds(pl.multiple_of(target * piece, 16), piece), :],
            part[u, pl.ds(pl.multiple_of(width + target * piece, 16), piece), :],
        )

    def opened(slot):
        scale = jnp.exp(slot[2 * piece:, :].astype(i32).astype(f32)[:1] * STEP) * (1.0 / TOP)
        return (
            slot[:piece, :].astype(i32).astype(f32) * scale,
            slot[piece:2 * piece, :].astype(i32).astype(f32) * scale,
        )

    def packed(slot, g, v):
        top = jnp.maximum(jnp.max(jnp.abs(g), axis=0, keepdims=True), jnp.max(jnp.abs(v), axis=0, keepdims=True))
        grade = jnp.ceil(jnp.log(jnp.maximum(top, 1e-30)) * (1.0 / STEP)) + 1.0
        up = jnp.exp(grade * -STEP) * TOP
        slot[:piece, :] = jnp.round(g * up).astype(i32).astype(i16)
        slot[piece:2 * piece, :] = jnp.round(v * up).astype(i32).astype(i16)
        slot[2 * piece:, :] = jnp.broadcast_to(grade.astype(i32), (16, lanes)).astype(i16)

    def sign(u):
        return 1 - 2 * lax.rem(u, 2)

    def far(u, hop):
        return remote(far_out.at[u, hop], far_in.at[u, hop], fs.at[u, hop], fr.at[u, hop],
                      at_device(lax.rem(z + sign(u) + RING, RING), core, row, col))

    def near(u, hop):
        return remote(near_out.at[u, hop], near_in.at[u, hop], ns.at[u, hop], nr.at[u, hop],
                      at_device(lax.rem(z - sign(u) + RING, RING), core, row, col))

    def pass_on(u, hop):
        g, v = own(u, lax.rem(z + sign(u) * (4 - hop) + RING, RING))
        if hop:
            far(u, hop - 1).wait_recv()
            a, b = opened(far_in.at[u, hop - 1])
            g, v = g + a, v + b
        packed(far_out.at[u, hop], g, v)
        far(u, hop).start()
        if hop < 3:
            g, v = own(u, lax.rem(z - sign(u) * (3 - hop) + RING, RING))
            if hop:
                near(u, hop - 1).wait_recv()
                a, b = opened(near_in.at[u, hop - 1])
                g, v = g + a, v + b
            packed(near_out.at[u, hop], g, v)
            near(u, hop).start()

    def scatter(t):
        return remote(kb.at[core * UNITS + t], k0.at[core * UNITS + t, rows_of(z)], ss.at[t], sr,
                      at_device(z, core, 2 * core + t // COLS, lax.rem(t, COLS)))

    def finish(u):
        g, v = own(u, z)
        near(u, 2).wait_recv()
        a, b = opened(near_in.at[u, 2])
        g, v = g + a, v + b
        far(u, 3).wait_recv()
        a, b = opened(far_in.at[u, 3])
        g, v = g + a, v + b
        t = spot_of(u)
        kb[core * UNITS + t] = (g * (1.0 / (1.0 + jnp.exp(-g))) * v).astype(bf16)
        home = jnp.logical_and(core == 0, t == 0)

        @pl.when(jnp.logical_and(origin, home))
        def _():
            k0[0, rows_of(z), :] = kb[0]

        @pl.when(jnp.logical_and(origin, jnp.logical_not(home)))
        def _():
            scatter(t).start()

    def weights_here(j, _):
        rows = tile(j * 128, 128)
        remote(wt.at[1 - core, rows], wt.at[1 - core, rows], ws.at[j], wr.at[j], partner).wait_recv()
        return 0

    lax.fori_loop(0, 2 * tiles, weights_here, 0)

    def step(g, _):
        for hop in range(1, 5):
            @pl.when(jnp.logical_and(g >= LAG * hop, g < UNITS + LAG * hop))
            def _(hop=hop):
                if hop < 4:
                    pass_on(g - LAG * hop, hop)
                else:
                    finish(g - LAG * hop)

        @pl.when(jnp.logical_and(lax.rem(g, 2) == 0, g < UNITS))
        def _():
            project(g // 2)

        @pl.when(g < UNITS)
        def _():
            pass_on(g, 0)

        return 0

    lax.fori_loop(0, UNITS + 4 * LAG, step, 0)

    own_keys = kb.at[pl.ds(core * UNITS, UNITS)]
    pair = remote(own_keys, own_keys, ps, pr, partner)
    pair.start()
    n, tokens = k0.shape[1], 2 * UNITS * lanes
    half_rows = n // 2

    def along(dz):
        here = k0.at[core * UNITS + first, rows_of(z)]
        return remote(here, here, zs.at[dz - 1], zr.at[dz - 1], at_device(lax.rem(z + dz, RING), core, row, col))

    def half_of(t, half):
        return k0.at[core * UNITS + t, pl.ds(half * half_rows, half_rows)]

    def block_first(half, step):
        here = half_of(first, half)
        return remote(here, here, b1.at[half, step - 1], br.at[first, half], in_row(step) if half else in_column(step))

    def block_row(s, step):
        t = s * COLS + col
        return remote(half_of(t, 0), half_of(t, 0), b2.at[s, step - 1], br.at[t, 0], in_row(step))

    def block_column(j, step):
        t = odd * COLS + lax.rem(col + j, COLS)
        return remote(half_of(t, 1), half_of(t, 1), b3.at[j, step - 1], br.at[t, 1], in_column(step))

    def quarter(t, half, part):
        return k0.at[core * UNITS + t, pl.ds(half * half_rows + part * (half_rows // 2), half_rows // 2)]

    def onward_row(s, part):
        t = s * COLS + lax.rem(col + (3, 1)[part], COLS)
        here = quarter(t, 0, part)
        return remote(here, here, c1.at[s, part], cr.at[t, 0, part], in_row((1, 3)[part]))

    def onward_column(s, j, part):
        t = s * COLS + j
        here = quarter(t, 1, part)
        return remote(here, here, c2.at[s, j], cr.at[t, 1, part], in_column((1, 3)[part]))

    def away(s):
        return lax.rem(row - 2 * core - s + 2 * ROWS, ROWS)

    def opposite(t, half):
        if half:
            return away(t // COLS) == 2
        return lax.rem(lax.rem(t, COLS) - col + COLS, COLS) == 2

    def here_block(t, half):
        remote(half_of(t, half), half_of(t, half), b1.at[0, 0], br.at[t, half], partner).wait_recv()

    @pl.when(holder)
    def _():
        @pl.when(jnp.logical_not(jnp.logical_and(origin, core == 0)))
        def _():
            here = k0.at[core * UNITS + first, rows_of(z)]
            remote(here, here, ss.at[0], sr, partner).wait_recv()

        for dz in range(1, RING):
            along(dz).start()

    for dz in range(1, RING):
        there = spots.at[core, lax.rem(z - dz + RING, RING)]
        remote(there, there, qs.at[dz - 1], qr.at[dz - 1], partner).wait_recv()
    over = remote(spots.at[core], spots.at[core], os, orr, partner)
    over.start()
    remote(spots.at[1 - core], spots.at[1 - core], os, orr, partner).wait_recv()
    over.wait_send()
    for dz in range(1, RING):
        spot_copy(dz).wait_send()

    lane = lax.broadcasted_iota(i32, (128, 128), 1)
    spots_row = jnp.concatenate([spots[group % 2, group // 2] for group in range(2 * RING)], axis=0).astype(i32)
    for b in range(2 * UNITS):
        select[b] = jnp.where(lane + b * lanes == spots_row, 1.0, 0.0).astype(bf16)
    m[...] = jnp.zeros((n, n), f32)
    grams[...] = jnp.zeros(grams.shape, f32)
    edit0[...] = jnp.zeros(edit0.shape, f32)
    edit[...] = jnp.zeros(edit.shape, f32)

    @pl.when(holder)
    def _():
        for dz in range(1, RING):
            there = k0.at[core * UNITS + first, rows_of(lax.rem(z - dz + RING, RING))]
            remote(there, there, zs.at[dz - 1], zr.at[dz - 1], partner).wait_recv()
        for step in (3, 1, 2):
            for half in range(2):
                block_first(half, step).start()

    for s in range(2):
        @pl.when(jnp.logical_not(jnp.logical_and(holder, odd == s)))
        def _(s=s):
            here_block(s * COLS + col, 0)
        for step in (1, 3):
            block_row(s, step).start()

    @pl.when(holder)
    def _():
        for j in range(COLS):
            if j:
                here_block(odd * COLS + lax.rem(col + j, COLS), 1)
            for step in (1, 3):
                block_column(j, step).start()

    for s in range(2):
        for part in range(2):
            here_block(s * COLS + lax.rem(col + (3, 1)[part], COLS), 0)
            onward_row(s, part).start()
    for s in range(2):
        for part in range(2):
            @pl.when(away(s) == (1, 3)[part])
            def _(s=s, part=part):
                for j in range(COLS):
                    here_block(s * COLS + j, 1)
                    onward_column(s, j, part).start()

    mid = n // 256 * 128 + 128
    nt = ((1,), (1,))

    def hand_over(c, t):
        here = k0.at[c * UNITS + t]
        return remote(here, here, hs.at[t], hr.at[t], partner)

    def add_pair(c, q):
        b0, b1_ = c * UNITS + spot_of(2 * q), c * UNITS + spot_of(2 * q + 1)
        a = jnp.concatenate([k0[b0], k0[b1_]], axis=1)
        own = jnp.concatenate([kb[b0], kb[b1_]], axis=1)
        hot = jnp.concatenate([select[b0], select[b1_]], axis=1)
        m[:mid, :] = m[:mid, :] + dot(a[:mid], a, nt)
        m[mid:, mid:] = m[mid:, mid:] + dot(a[mid:], a[mid:], nt)
        grams[...] = grams[...] + dot(own, a, nt)
        edit0[...] = edit0[...] + dot(a, hot, nt)
        edit[...] = edit[...] + dot(own, hot, nt)

    their_keys = kb.at[pl.ds((1 - core) * UNITS, UNITS)]
    remote(their_keys, their_keys, ps, pr, partner).wait_recv()

    def near_pair(q, _):
        for j in range(2):
            t = spot_of(2 * q + j)
            for half in range(2):
                @pl.when(opposite(t, half))
                def _(t=t, half=half):
                    for part in range(2):
                        here = quarter(t, half, part)
                        remote(here, here, c1.at[0, 0], cr.at[t, half, part], partner).wait_recv()
            hand_over(core, t).start()
        add_pair(core, q)
        return 0

    lax.fori_loop(0, UNITS // 2, near_pair, 0)

    def far_pair(q, _):
        for j in range(2):
            hand_over(1 - core, spot_of(2 * q + j)).wait_recv()
        add_pair(1 - core, q)
        return 0

    lax.fori_loop(0, UNITS // 2, far_pair, 0)

    share = 1.0 / tokens
    top = jnp.max(jnp.abs(grams[...]), axis=1, keepdims=True) * share
    grade = jnp.ceil(jnp.log(jnp.maximum(top, 1e-30)) * (1.0 / STEP)) + 1.0
    scaled = jnp.round(grams[...] * (jnp.exp(grade * -STEP) * (TOP * share))).astype(i32).astype(i16)
    half = g_all.shape[3]

    @pl.when(core == 0)
    def _():
        g_all[0, z] = scaled[:, :half]

    @pl.when(core == 1)
    def _():
        g_all[1, z, :, :n - half] = scaled[:, half:]
        g_all[1, z, :, n - half:] = jnp.broadcast_to(grade.astype(i32), (piece, 2 * half - n)).astype(i16)

    e_all[z] = edit[...].astype(bf16)

    def give(dz):
        there = at_device(lax.rem(z + dz, RING), core, row, col)
        g, e = g_all.at[core, z], e_all.at[z]
        return (remote(g, g, gs.at[dz - 1], gr.at[dz - 1], there), remote(e, e, es.at[dz - 1], er.at[dz - 1], there))

    def take(dz):
        source = lax.rem(z - dz + RING, RING)
        g, e = g_all.at[core, source], e_all.at[source]
        return (remote(g, g, gs.at[dz - 1], gr.at[dz - 1], partner), remote(e, e, es.at[dz - 1], er.at[dz - 1], partner))

    for dz in range(1, RING):
        for copy in give(dz):
            copy.start()
    give_over = remote(g_all.at[core], g_all.at[core], vs, vr, partner)

    blocks = n // 128
    r_i = lax.broadcasted_iota(i32, (128, 128), 0)
    c_i = lax.broadcasted_iota(i32, (128, 128), 1)
    m[...] = m[...] * share
    for k in range(blocks):
        at = slice(k * 128, (k + 1) * 128)
        m[at, at] = m[at, at] + jnp.where(r_i == c_i, jnp.broadcast_to(regular[at], (128, 128)), 0.0)
    l_out[...] = jnp.zeros((n, n), f32)

    def step(k, _):
        at = pl.ds(pl.multiple_of(k * 128, 128), 128)

        def load(i):
            return m[pl.ds(pl.multiple_of(k * 128 + 8 * i, 8), 8), at]

        def store(i, a, v):
            up[8 * i:8 * i + 8, :] = a
            inv[8 * i:8 * i + 8, :] = v

        factor_block(load, store)
        l_out[at, at] = up[...].T

        @pl.when(k == blocks - 2)
        def _():
            for dz in range(1, RING):
                for copy in take(dz):
                    copy.wait_recv()
            give_over.start()

        for fixed in range(blocks):
            @pl.when(k == fixed)
            def _(fixed=fixed):
                lo, hi = fixed * 128, (fixed + 1) * 128
                li = inv[...]
                if fixed:
                    m[lo:hi, :lo] = dot(li, m[lo:hi, :lo], ((1,), (0,)), HI)
                m[lo:hi, lo:hi] = li
                if hi < n:
                    m[lo:hi, hi:] = dot(li, m[lo:hi, hi:], ((1,), (0,)), HI)
                    lt = m[lo:hi, hi:].T
                    l_out[hi:, lo:hi] = lt
                    for rlo in range(hi, n, 128):
                        rows = slice(rlo, rlo + 128)
                        cut = lt[rlo - hi:rlo - hi + 128]
                        if fixed:
                            m[rows, :lo] = m[rows, :lo] - dot(cut, m[lo:hi, :lo], ((1,), (0,)), HI)
                        m[rows, lo:hi] = -dot(cut, li, ((1,), (0,)), HI)
                        m[rows, rlo:] = m[rows, rlo:] - dot(cut, m[lo:hi, rlo:], ((1,), (0,)), HI)
        return 0

    lax.fori_loop(0, blocks, step, 0)
    for k in range(blocks - 1):
        lo, hi = k * 128, (k + 1) * 128
        m[lo:hi, hi:] = jnp.zeros((128, n - hi), f32)
    solved = dot(m[...], edit0[...], ((1,), (0,)), HI)
    edit0[...] = solved
    whole, rest = split(m[...])
    inv_hi[...] = whole
    inv_lo[...] = rest
    remote(g_all.at[1 - core], g_all.at[1 - core], vs, vr, partner).wait_recv()
    nn = ((1,), (0,))

    def send(rows, weight):
        a, b = split(weight)
        u_out[rows, :] = dot(a, res[...], nn) + dot(b, res[...], nn)

    @pl.when(origin)
    def _():
        send(pl.ds(0, n), edit0[...])

    @pl.when(jnp.logical_not(origin))
    def _():
        c, d = split(edit0[...])

        def rows_part(i, _):
            rows = tile(i * 4 * piece, 4 * piece)
            g = jnp.concatenate([
                jnp.concatenate([g_all[0, 4 * i + s], g_all[1, 4 * i + s]], axis=1) for s in range(4)
            ], axis=0).astype(i32)
            scale = jnp.exp(g[:, n:n + 1].astype(f32) * STEP) * (1.0 / TOP)
            g = g[:, :n]
            high = lax.shift_right_arithmetic(g, 8)
            low = (g - high * 256).astype(f32).astype(bf16)
            high = high.astype(f32).astype(bf16)
            for lo in range(0, n, 256):
                hi = min(lo + 256, n)
                at = slice(lo, hi)
                a, b = inv_hi[at, :hi], inv_lo[at, :hi]
                big = dot(high[:, :hi], a, nt) + dot(high[:, :hi], b, nt)
                l_out[rows, at] = (big * 256.0 + dot(low[:, :hi], a, nt)) * scale
            a, b = split(l_out[rows, :])
            ends = jnp.concatenate([e_all[4 * i + s] for s in range(4)], axis=0).astype(f32)
            send(rows, ends - (dot(a, c, nn) + dot(a, d, nn) + dot(b, c, nn)))
            return 0

        lax.fori_loop(0, RING // 4, rows_part, 0)

    give_over.wait_send()
    for dz in range(1, RING):
        for copy in give(dz):
            copy.wait_send()
    pair.wait_send()
    for t in range(UNITS):
        hand_over(core, t).wait_send()

    @pl.when(origin)
    def _():
        for t in range(UNITS):
            if t == 0:
                @pl.when(core == 1)
                def _():
                    scatter(0).wait_send()
            else:
                scatter(t).wait_send()

    for step in (1, 2, 3):
        token_first(step).wait_send()
        for s in range(2):
            token_row(s, step).wait_send()
            if step != 2:
                block_row(s, step).wait_send()

    @pl.when(core != mine)
    def _():
        token_first(0).wait_send()

    @pl.when(holder)
    def _():
        for dz in range(1, RING):
            along(dz).wait_send()
        for step in (1, 2, 3):
            for half in range(2):
                block_first(half, step).wait_send()
            for j in range(COLS):
                token_column(j, step).wait_send()
                if step != 2:
                    block_column(j, step).wait_send()

    for s in range(2):
        for part in range(2):
            onward_row(s, part).wait_send()

            @pl.when(away(s) == (1, 3)[part])
            def _(s=s, part=part):
                for j in range(COLS):
                    onward_column(s, j, part).wait_send()

    def sent(j, _):
        weight_copy(j).wait_send()
        return 0

    lax.fori_loop(0, 2 * tiles, sent, 0)

    def ring_sent(u, _):
        for hop in range(4):
            far(u, hop).wait_send()
            if hop < 3:
                near(u, hop).wait_send()
        return 0

    lax.fori_loop(0, UNITS, ring_sent, 0)


def split(a):
    whole = a.astype(bf16)
    return whole, (a - whole.astype(f32)).astype(bf16)


def whole_call(tok, wg, wu, lengths, raw, regular, res):
    lanes, depth = tok.shape
    width = wg.shape[1]
    piece = width // RING
    rows = 2 * piece + 16
    n, blocks, facts = width, 2 * UNITS, 8 * 2 * RING
    dma = pltpu.SemaphoreType.DMA
    vmem = pl.BlockSpec(memory_space=pltpu.VMEM)
    tiles = 2 * width // 128
    return pl.pallas_call(
        whole_kernel,
        out_shape=[jax.ShapeDtypeStruct((n, n), f32), jax.ShapeDtypeStruct((n, res.shape[1]), f32)],
        in_specs=[pl.BlockSpec(memory_space=pl.ANY)] * 3 + [vmem] * 4,
        out_specs=[vmem] * 2,
        scratch_shapes=[
            pltpu.VMEM((lanes, depth), bf16),
            pltpu.VMEM((depth, width), bf16),
            pltpu.VMEM((depth, width), bf16),
            pltpu.VMEM((2, RING, 8, 128), f32),
            pltpu.VMEM((UNITS, 2, lanes, depth), bf16),
            pltpu.VMEM((2, 2 * width, depth), bf16),
            pltpu.VMEM((UNITS, 2 * width, lanes), f32),
            pltpu.VMEM((UNITS, 4, rows, lanes), i16),
            pltpu.VMEM((UNITS, 4, rows, lanes), i16),
            pltpu.VMEM((UNITS, 3, rows, lanes), i16),
            pltpu.VMEM((UNITS, 3, rows, lanes), i16),
            pltpu.VMEM((blocks, n, lanes), bf16),
            pltpu.VMEM((blocks, piece, lanes), bf16),
            pltpu.VMEM((blocks, facts, lanes), bf16),
            pltpu.VMEM((n, n), f32),
            pltpu.VMEM((128, 128), f32),
            pltpu.VMEM((128, 128), f32),
            pltpu.VMEM((piece, n), f32),
            pltpu.VMEM((n, facts), f32),
            pltpu.VMEM((piece, facts), f32),
            pltpu.VMEM((2, RING, piece, 512), i16),
            pltpu.VMEM((RING, piece, facts), bf16),
            pltpu.VMEM((n, n), bf16),
            pltpu.VMEM((n, n), bf16),
            dma((3,)), dma((RING - 1,)), dma((RING - 1,)), dma, dma,
            dma((4,)), dma((2, 3)), dma((COLS, 3)), dma((UNITS, 2)), dma((tiles,)), dma((tiles,)),
            dma((UNITS, 4)), dma((UNITS, 4)), dma((UNITS, 3)), dma((UNITS, 3)),
            dma, dma, dma((UNITS,)), dma, dma((RING - 1,)), dma((RING - 1,)),
            dma((2, 3)), dma((2, 3)), dma((COLS, 3)), dma((UNITS, 2)),
            dma((2, 2)), dma((2, COLS)), dma((UNITS, 2, 2)), dma((UNITS,)), dma((UNITS,)),
            dma((RING - 1,)), dma((RING - 1,)), dma((RING - 1,)), dma((RING - 1,)), dma, dma,
        ],
        compiler_params=pltpu.CompilerParams(collective_id=0, has_side_effects=True, vmem_limit_bytes=60 << 20),
        name="panel_edit",
    )(tok, wg, wu, lengths, raw, regular, res)


def on_device(tokens_in, gate_weight, up_weight, doc_lengths, subject_raw, residuals, regular):
    return tuple(whole_call(tokens_in, gate_weight, up_weight, doc_lengths, subject_raw, regular, residuals))


def solution(mesh):
    return jax.shard_map(
        on_device,
        mesh=mesh,
        in_specs=(
            P(("row", "col"), "doc"),
            P("doc", ("row", "col")),
            P("doc", ("row", "col")),
            P("doc", None),
            P("doc", None),
            P(None, "doc"),
            P(),
        ),
        out_specs=(P(("row", "col"), None), P(("row", "col"), "doc")),
        check_vma=False,
    )
```

```python
import functools
import math

import jax
import jax.numpy as jnp
from jax import lax
from jax.experimental import pallas as pl
from jax.experimental.pallas import tpu as pltpu
from jax.sharding import PartitionSpec as P

HI = lax.Precision.HIGHEST
MESH = pl.DeviceIdType.MESH
f32, bf16, i16, i32 = jnp.float32, jnp.bfloat16, jnp.int16, jnp.int32

ROWS, COLS, RING = 4, 4, 8
UNITS = 8
LAG = 3
LN2 = math.log(2.0)
STEP = LN2 / 64
TOP = 32700.0


def dot(a, b, dims, precision=None):
    return lax.dot_general(a, b, (dims, ((), ())), precision=precision, preferred_element_type=f32)


def spread_row(v, k):
    return jnp.broadcast_to(v[k:k + 1, :], v.shape)


def spread_lane(v, j):
    return jnp.broadcast_to(v[:, j:j + 1], v.shape)


def factor_block(load, store):
    sub = lax.broadcasted_iota(jnp.int32, (8, 128), 0)
    lane = lax.broadcasted_iota(jnp.int32, (8, 128), 1)
    left = [load(i) for i in range(16)]
    right = [jnp.where(lane == sub + 8 * i, 1.0, 0.0).astype(f32) for i in range(16)]
    for p in range(16):
        cols = [spread_lane(left[p], 8 * p + k) for k in range(8)]
        below = {i: [spread_lane(left[i], 8 * p + k) for k in range(8)] for i in range(p + 1, 16)}
        pivots = jnp.zeros((8, 128), f32)
        a, v = left[p], right[p]
        for k in range(8):
            pivot = spread_row(cols[k], k)
            inv = 1.0 / pivot
            pivots = jnp.where(sub == k, pivot, pivots)
            ak, vk = spread_row(a, k), spread_row(v, k)
            lead = {m: spread_row(cols[m], k) for m in range(k + 1, 8)}
            mult = jnp.where(sub > k, cols[k] * inv, 0.0)
            for m in range(k + 1, 8):
                cols[m] = cols[m] - mult * lead[m]
            a = a - mult * ak
            v = v - mult * vk
            for i in range(p + 1, 16):
                part = below[i][k] * inv
                for m in range(k + 1, 8):
                    below[i][m] = below[i][m] - part * lead[m]
                left[i] = left[i] - part * ak
                right[i] = right[i] - part * vk
        scale = lax.rsqrt(pivots)
        store(p, jnp.where(lane >= sub + 8 * p, a * scale, 0.0), v * scale)


def place():
    doc = lax.axis_index("doc")
    return doc // 2, lax.rem(doc, 2), lax.axis_index("row"), lax.axis_index("col")


def at_device(z, core, row, col):
    return {"doc": z * 2 + core, "row": row, "col": col}


def greet(z, core, row, col, ring_steps):
    barrier = pltpu.get_barrier_semaphore()
    count = 0
    for dr in range(ROWS):
        for dc in range(COLS):
            for other in range(2):
                if dr == 0 and dc == 0 and other == 0:
                    continue
                device = at_device(z, lax.rem(core + other, 2), lax.rem(row + dr, ROWS), lax.rem(col + dc, COLS))
                pl.semaphore_signal(barrier, inc=1, device_id=device, device_id_type=MESH)
                count += 1
    for step in ring_steps:
        pl.semaphore_signal(barrier, inc=1, device_id=at_device(lax.rem(z + step, RING), core, row, col), device_id_type=MESH)
        count += 1
    return barrier, count


def remote(src, dst, send, recv, device):
    return pltpu.make_async_remote_copy(
        src_ref=src, dst_ref=dst, send_sem=send, recv_sem=recv, device_id=device, device_id_type=MESH
    )


def tile(start, size):
    return pl.ds(pl.multiple_of(start, size), size)


def whole_kernel(tok_ref, wg_ref, wu_ref, lengths_ref, raw_ref, regular, res, l_out, u_out,
                 tok, wg, wu, spots, xg, wt, part, far_out, far_in, near_out, near_in,
                 k0, kb, select, m, up, inv, grams, edit0, edit, g_all, e_all, inv_hi, inv_lo,
                 ls, qs, qr, os, orr, t1, t2, t3, xr, ws, wr, fs, fr, ns, nr,
                 ps, pr, ss, sr, zs, zr, b1, b2, b3, br, c1, c2, cr, hs, hr, gs, gr, es, er, vs, vr):
    z, core, row, col = place()
    loads = [pltpu.make_async_copy(a, b, ls.at[i]) for i, (a, b) in enumerate(((tok_ref, tok), (wg_ref, wg), (wu_ref, wu)))]
    for load in loads:
        load.start()
    depth, width = wg.shape
    piece = width // RING
    lanes = tok.shape[0]
    odd = lax.rem(row, 2)
    first = odd * COLS + col
    mine = row // 2
    holder = core == mine
    origin = jnp.logical_and(row == 0, col == 0)

    def rows_of(zz):
        return pl.ds(pl.multiple_of(zz * piece, 16), piece)

    def in_row(step):
        return at_device(z, core, row, lax.rem(col + step, COLS))

    def in_column(step):
        return at_device(z, core, lax.rem(row + step, ROWS), col)

    barrier, count = greet(z, core, row, col, tuple(range(1, RING)))
    sub = lax.broadcasted_iota(i32, (8, 128), 0)
    square = lax.broadcasted_iota(i32, (8, 8), 0) == lax.broadcasted_iota(i32, (8, 8), 1)

    def upright(ref):
        values = jnp.broadcast_to(ref[...].astype(f32), (8, 8))
        return jnp.broadcast_to(jnp.sum(jnp.where(square, values, 0.0), axis=1, keepdims=True), (8, 128))

    lengths, raw = upright(lengths_ref), upright(raw_ref)
    starts = jnp.zeros((8, 128), f32)
    for j in range(7):
        starts = starts + jnp.where(sub > j, jnp.broadcast_to(lengths[j:j + 1, :], (8, 128)), 0.0)
    wrapped = raw - lengths * jnp.floor((raw + 0.5) / lengths)
    spots[core, z] = starts + wrapped + ((z * 2 + core) * lanes).astype(f32)

    @pl.when(holder)
    def _():
        for step in range(1, RING):
            pl.semaphore_signal(barrier, inc=1, device_id=at_device(lax.rem(z + step, RING), core, 0, 0), device_id_type=MESH)

    pl.semaphore_wait(barrier, count + jnp.where(origin, (RING - 1) * UNITS, 0))

    def spot_copy(dz):
        here = spots.at[core, z]
        return remote(here, here, qs.at[dz - 1], qr.at[dz - 1], at_device(lax.rem(z + dz, RING), core, row, col))

    loads[0].wait()

    def token_first(step):
        slot = xg.at[first, core]
        x_way = at_device(z, mine, lax.rem(row + step * (1 - core), ROWS), lax.rem(col + step * core, COLS))
        return remote(tok, slot, t1.at[step], xr.at[first, core], x_way)

    for step in (0, 3, 2, 1):
        if step:
            token_first(step).start()
        else:
            @pl.when(core != mine)
            def _():
                token_first(0).start()

    @pl.when(holder)
    def _():
        xg[first, core] = tok[...]

    partner = at_device(z, 1 - core, row, col)

    def weight_copy(j):
        rows = tile(j * 128, 128)
        return remote(wt.at[core, rows], wt.at[core, rows], ws.at[j], wr.at[j], partner)

    tiles = width // 128
    loads[1].wait()
    loads[2].wait()

    def turn(j, _):
        at = tile(j * 128, 128)
        wt[core, at, :] = wg[:, at].T
        weight_copy(j).start()
        wt[core, tile((j + tiles) * 128, 128), :] = wu[:, at].T
        weight_copy(j + tiles).start()
        return 0

    def here_tokens(t, half):
        slot = xg.at[t, half]
        remote(slot, slot, t1.at[0], xr.at[t, half], partner).wait_recv()

    def token_row(s, step):
        slot = xg.at[s * COLS + col, 0]
        return remote(slot, slot, t2.at[s, step - 1], xr.at[s * COLS + col, 0], in_row(step))

    def token_column(j, step):
        t = odd * COLS + lax.rem(col + j, COLS)
        return remote(xg.at[t, 1], xg.at[t, 1], t3.at[j, step - 1], xr.at[t, 1], in_column(step))

    lax.fori_loop(0, 3, turn, 0)
    for s in range(2):
        @pl.when(jnp.logical_not(jnp.logical_and(holder, jnp.logical_and(core == 0, odd == s))))
        def _(s=s):
            here_tokens(s * COLS + col, 0)
        for step in (3, 2, 1):
            token_row(s, step).start()

    @pl.when(holder)
    def _():
        for j in range(COLS):
            if j == 0:
                @pl.when(core == 0)
                def _():
                    here_tokens(first, 1)
            else:
                here_tokens(odd * COLS + lax.rem(col + j, COLS), 1)
            for step in (1, 3, 2):
                token_column(j, step).start()

    lax.fori_loop(3, tiles, turn, 0)
    for dz in range(1, RING):
        spot_copy(dz).start()

    def spot_of(u):
        return lax.rem(u, 2) * COLS + lax.rem(col + u // 2, COLS)

    def settled(t, half):
        if half == 0:
            return lax.rem(t, COLS) == col
        return jnp.logical_and(holder, t // COLS == odd)

    def wait_tokens(u):
        for half in range(2):
            @pl.when(jnp.logical_not(settled(spot_of(u), half)))
            def _(half=half):
                here_tokens(spot_of(u), half)

    def project(pair):
        wait_tokens(2 * pair)
        wait_tokens(2 * pair + 1)
        x = [jnp.concatenate([xg[spot_of(2 * pair), half], xg[spot_of(2 * pair + 1), half]], axis=0) for half in range(2)]

        def chunk(j, _):
            rows = tile(j * 448, 448)
            total = dot(wt[0, rows, :], x[0], ((1,), (1,))) + dot(wt[1, rows, :], x[1], ((1,), (1,)))
            part[2 * pair, rows, :] = total[:, :lanes]
            part[2 * pair + 1, rows, :] = total[:, lanes:]
            return 0

        lax.fori_loop(0, 2 * width // 448, chunk, 0)

    def own(u, target):
        return (
            part[u, pl.ds(pl.multiple_of(target * piece, 16), piece), :],
            part[u, pl.ds(pl.multiple_of(width + target * piece, 16), piece), :],
        )

    def opened(slot):
        scale = jnp.exp(slot[2 * piece:, :].astype(i32).astype(f32)[:1] * STEP) * (1.0 / TOP)
        return (
            slot[:piece, :].astype(i32).astype(f32) * scale,
            slot[piece:2 * piece, :].astype(i32).astype(f32) * scale,
        )

    def packed(slot, g, v):
        top = jnp.maximum(jnp.max(jnp.abs(g), axis=0, keepdims=True), jnp.max(jnp.abs(v), axis=0, keepdims=True))
        grade = jnp.ceil(jnp.log(jnp.maximum(top, 1e-30)) * (1.0 / STEP)) + 1.0
        up = jnp.exp(grade * -STEP) * TOP
        slot[:piece, :] = jnp.round(g * up).astype(i32).astype(i16)
        slot[piece:2 * piece, :] = jnp.round(v * up).astype(i32).astype(i16)
        slot[2 * piece:, :] = jnp.broadcast_to(grade.astype(i32), (16, lanes)).astype(i16)

    def sign(u):
        return 1 - 2 * lax.rem(u, 2)

    def far(u, hop):
        return remote(far_out.at[u, hop], far_in.at[u, hop], fs.at[u, hop], fr.at[u, hop],
                      at_device(lax.rem(z + sign(u) + RING, RING), core, row, col))

    def near(u, hop):
        return remote(near_out.at[u, hop], near_in.at[u, hop], ns.at[u, hop], nr.at[u, hop],
                      at_device(lax.rem(z - sign(u) + RING, RING), core, row, col))

    def pass_on(u, hop):
        g, v = own(u, lax.rem(z + sign(u) * (4 - hop) + RING, RING))
        if hop:
            far(u, hop - 1).wait_recv()
            a, b = opened(far_in.at[u, hop - 1])
            g, v = g + a, v + b
        packed(far_out.at[u, hop], g, v)
        far(u, hop).start()
        if hop < 3:
            g, v = own(u, lax.rem(z - sign(u) * (3 - hop) + RING, RING))
            if hop:
                near(u, hop - 1).wait_recv()
                a, b = opened(near_in.at[u, hop - 1])
                g, v = g + a, v + b
            packed(near_out.at[u, hop], g, v)
            near(u, hop).start()

    def scatter(t, dz):
        return remote(kb.at[core * UNITS + t], k0.at[core * UNITS + t, rows_of(z)], ss.at[t, dz], zr.at[dz],
                      at_device(lax.rem(z + dz, RING), core, 2 * core + t // COLS, lax.rem(t, COLS)))

    def finish(u):
        g, v = own(u, z)
        near(u, 2).wait_recv()
        a, b = opened(near_in.at[u, 2])
        g, v = g + a, v + b
        far(u, 3).wait_recv()
        a, b = opened(far_in.at[u, 3])
        g, v = g + a, v + b
        t = spot_of(u)
        kb[core * UNITS + t] = (g * (1.0 / (1.0 + jnp.exp(-g))) * v).astype(bf16)
        home = jnp.logical_and(core == 0, t == 0)

        @pl.when(jnp.logical_and(origin, home))
        def _():
            k0[0, rows_of(z), :] = kb[0]

        @pl.when(jnp.logical_and(origin, jnp.logical_not(home)))
        def _():
            scatter(t, 0).start()

        @pl.when(origin)
        def _():
            for dz in range(1, RING):
                scatter(t, dz).start()

    def weights_here(j, _):
        rows = tile(j * 128, 128)
        remote(wt.at[1 - core, rows], wt.at[1 - core, rows], ws.at[j], wr.at[j], partner).wait_recv()
        return 0

    lax.fori_loop(0, 2 * tiles, weights_here, 0)

    def step(g, _):
        for hop in range(1, 5):
            @pl.when(jnp.logical_and(g >= LAG * hop, g < UNITS + LAG * hop))
            def _(hop=hop):
                if hop < 4:
                    pass_on(g - LAG * hop, hop)
                else:
                    finish(g - LAG * hop)

        @pl.when(jnp.logical_and(lax.rem(g, 2) == 0, g < UNITS))
        def _():
            project(g // 2)

        @pl.when(g < UNITS)
        def _():
            pass_on(g, 0)

        return 0

    lax.fori_loop(0, UNITS + 4 * LAG, step, 0)

    own_keys = kb.at[pl.ds(core * UNITS, UNITS)]
    pair = remote(own_keys, own_keys, ps, pr, partner)
    pair.start()
    n, tokens = k0.shape[1], 2 * UNITS * lanes
    half_rows = n // 2

    def half_of(t, half):
        return k0.at[core * UNITS + t, pl.ds(half * half_rows, half_rows)]

    def block_first(half, step):
        here = half_of(first, half)
        return remote(here, here, b1.at[half, step - 1], br.at[first, half], in_row(step) if half else in_column(step))

    def block_row(s, step):
        t = s * COLS + col
        return remote(half_of(t, 0), half_of(t, 0), b2.at[s, step - 1], br.at[t, 0], in_row(step))

    def block_column(j, step):
        t = odd * COLS + lax.rem(col + j, COLS)
        return remote(half_of(t, 1), half_of(t, 1), b3.at[j, step - 1], br.at[t, 1], in_column(step))

    def quarter(t, half, part):
        return k0.at[core * UNITS + t, pl.ds(half * half_rows + part * (half_rows // 2), half_rows // 2)]

    def onward_row(s, part):
        t = s * COLS + lax.rem(col + (3, 1)[part], COLS)
        here = quarter(t, 0, part)
        return remote(here, here, c1.at[s, part], cr.at[t, 0, part], in_row((1, 3)[part]))

    def onward_column(s, j, part):
        t = s * COLS + j
        here = quarter(t, 1, part)
        return remote(here, here, c2.at[s, j], cr.at[t, 1, part], in_column((1, 3)[part]))

    def away(s):
        return lax.rem(row - 2 * core - s + 2 * ROWS, ROWS)

    def opposite(t, half):
        if half:
            return away(t // COLS) == 2
        return lax.rem(lax.rem(t, COLS) - col + COLS, COLS) == 2

    def here_block(t, half):
        remote(half_of(t, half), half_of(t, half), b1.at[0, 0], br.at[t, half], partner).wait_recv()

    for dz in range(1, RING):
        there = spots.at[core, lax.rem(z - dz + RING, RING)]
        remote(there, there, qs.at[dz - 1], qr.at[dz - 1], partner).wait_recv()
    over = remote(spots.at[core], spots.at[core], os, orr, partner)
    over.start()
    remote(spots.at[1 - core], spots.at[1 - core], os, orr, partner).wait_recv()
    over.wait_send()
    for dz in range(1, RING):
        spot_copy(dz).wait_send()

    lane = lax.broadcasted_iota(i32, (128, 128), 1)
    spots_row = jnp.concatenate([spots[group % 2, group // 2] for group in range(2 * RING)], axis=0).astype(i32)
    for b in range(2 * UNITS):
        select[b] = jnp.where(lane + b * lanes == spots_row, 1.0, 0.0).astype(bf16)
    m[...] = jnp.zeros((n, n), f32)
    grams[...] = jnp.zeros(grams.shape, f32)
    edit0[...] = jnp.zeros(edit0.shape, f32)
    edit[...] = jnp.zeros(edit.shape, f32)

    @pl.when(holder)
    def _():
        def piece_here(dz):
            there = k0.at[core * UNITS + first, rows_of(lax.rem(z - dz + RING, RING))]
            remote(there, there, zs.at[0], zr.at[dz], partner).wait_recv()

        @pl.when(jnp.logical_not(jnp.logical_and(origin, core == 0)))
        def _():
            piece_here(0)

        for dz in range(1, RING):
            piece_here(dz)
        for step in (3, 1, 2):
            for half in range(2):
                block_first(half, step).start()

    for s in range(2):
        @pl.when(jnp.logical_not(jnp.logical_and(holder, odd == s)))
        def _(s=s):
            here_block(s * COLS + col, 0)
        for step in (1, 3):
            block_row(s, step).start()

    @pl.when(holder)
    def _():
        for j in range(COLS):
            if j:
                here_block(odd * COLS + lax.rem(col + j, COLS), 1)
            for step in (1, 3):
                block_column(j, step).start()

    for s in range(2):
        for part in range(2):
            here_block(s * COLS + lax.rem(col + (3, 1)[part], COLS), 0)
            onward_row(s, part).start()
    for s in range(2):
        for part in range(2):
            @pl.when(away(s) == (1, 3)[part])
            def _(s=s, part=part):
                for j in range(COLS):
                    here_block(s * COLS + j, 1)
                    onward_column(s, j, part).start()

    mid = n // 256 * 128 + 128
    nt = ((1,), (1,))

    def hand_over(c, t):
        here = k0.at[c * UNITS + t]
        return remote(here, here, hs.at[t], hr.at[t], partner)

    def add_pair(c, q):
        b0, b1_ = c * UNITS + spot_of(2 * q), c * UNITS + spot_of(2 * q + 1)
        a = jnp.concatenate([k0[b0], k0[b1_]], axis=1)
        own = jnp.concatenate([kb[b0], kb[b1_]], axis=1)
        hot = jnp.concatenate([select[b0], select[b1_]], axis=1)
        m[:mid, :] = m[:mid, :] + dot(a[:mid], a, nt)
        m[mid:, mid:] = m[mid:, mid:] + dot(a[mid:], a[mid:], nt)
        grams[...] = grams[...] + dot(own, a, nt)
        edit0[...] = edit0[...] + dot(a, hot, nt)
        edit[...] = edit[...] + dot(own, hot, nt)

    their_keys = kb.at[pl.ds((1 - core) * UNITS, UNITS)]
    remote(their_keys, their_keys, ps, pr, partner).wait_recv()

    def near_pair(q, _):
        for j in range(2):
            t = spot_of(2 * q + j)
            for half in range(2):
                @pl.when(opposite(t, half))
                def _(t=t, half=half):
                    for part in range(2):
                        here = quarter(t, half, part)
                        remote(here, here, c1.at[0, 0], cr.at[t, half, part], partner).wait_recv()
            hand_over(core, t).start()
        add_pair(core, q)
        return 0

    lax.fori_loop(0, UNITS // 2, near_pair, 0)

    def far_pair(q, _):
        for j in range(2):
            hand_over(1 - core, spot_of(2 * q + j)).wait_recv()
        add_pair(1 - core, q)
        return 0

    lax.fori_loop(0, UNITS // 2, far_pair, 0)

    share = 1.0 / tokens
    top = jnp.max(jnp.abs(grams[...]), axis=1, keepdims=True) * share
    grade = jnp.ceil(jnp.log(jnp.maximum(top, 1e-30)) * (1.0 / STEP)) + 1.0
    scaled = jnp.round(grams[...] * (jnp.exp(grade * -STEP) * (TOP * share))).astype(i32).astype(i16)
    half = g_all.shape[3]

    @pl.when(core == 0)
    def _():
        g_all[0, z] = scaled[:, :half]

    @pl.when(core == 1)
    def _():
        g_all[1, z, :, :n - half] = scaled[:, half:]
        g_all[1, z, :, n - half:] = jnp.broadcast_to(grade.astype(i32), (piece, 2 * half - n)).astype(i16)

    e_all[z] = edit[...].astype(bf16)

    def give(dz):
        there = at_device(lax.rem(z + dz, RING), core, row, col)
        g, e = g_all.at[core, z], e_all.at[z]
        return (remote(g, g, gs.at[dz - 1], gr.at[dz - 1], there), remote(e, e, es.at[dz - 1], er.at[dz - 1], there))

    def take(dz):
        source = lax.rem(z - dz + RING, RING)
        g, e = g_all.at[core, source], e_all.at[source]
        return (remote(g, g, gs.at[dz - 1], gr.at[dz - 1], partner), remote(e, e, es.at[dz - 1], er.at[dz - 1], partner))

    for dz in range(1, RING):
        for copy in give(dz):
            copy.start()
    give_over = remote(g_all.at[core], g_all.at[core], vs, vr, partner)

    blocks = n // 128
    r_i = lax.broadcasted_iota(i32, (128, 128), 0)
    c_i = lax.broadcasted_iota(i32, (128, 128), 1)
    m[...] = m[...] * share
    for k in range(blocks):
        at = slice(k * 128, (k + 1) * 128)
        m[at, at] = m[at, at] + jnp.where(r_i == c_i, jnp.broadcast_to(regular[at], (128, 128)), 0.0)
    l_out[...] = jnp.zeros((n, n), f32)

    def step(k, _):
        at = pl.ds(pl.multiple_of(k * 128, 128), 128)

        def load(i):
            return m[pl.ds(pl.multiple_of(k * 128 + 8 * i, 8), 8), at]

        def store(i, a, v):
            up[8 * i:8 * i + 8, :] = a
            inv[8 * i:8 * i + 8, :] = v

        factor_block(load, store)
        l_out[at, at] = up[...].T

        @pl.when(k == blocks - 2)
        def _():
            for dz in range(1, RING):
                for copy in take(dz):
                    copy.wait_recv()
            give_over.start()

        for fixed in range(blocks):
            @pl.when(k == fixed)
            def _(fixed=fixed):
                lo, hi = fixed * 128, (fixed + 1) * 128
                li = inv[...]
                if fixed:
                    m[lo:hi, :lo] = dot(li, m[lo:hi, :lo], ((1,), (0,)), HI)
                m[lo:hi, lo:hi] = li
                if hi < n:
                    m[lo:hi, hi:] = dot(li, m[lo:hi, hi:], ((1,), (0,)), HI)
                    lt = m[lo:hi, hi:].T
                    l_out[hi:, lo:hi] = lt
                    for rlo in range(hi, n, 128):
                        rows = slice(rlo, rlo + 128)
                        cut = lt[rlo - hi:rlo - hi + 128]
                        if fixed:
                            m[rows, :lo] = m[rows, :lo] - dot(cut, m[lo:hi, :lo], ((1,), (0,)), HI)
                        m[rows, lo:hi] = -dot(cut, li, ((1,), (0,)), HI)
                        m[rows, rlo:] = m[rows, rlo:] - dot(cut, m[lo:hi, rlo:], ((1,), (0,)), HI)
        return 0

    lax.fori_loop(0, blocks, step, 0)
    for k in range(blocks - 1):
        lo, hi = k * 128, (k + 1) * 128
        m[lo:hi, hi:] = jnp.zeros((128, n - hi), f32)
    solved = dot(m[...], edit0[...], ((1,), (0,)), HI)
    edit0[...] = solved
    whole, rest = split(m[...])
    inv_hi[...] = whole
    inv_lo[...] = rest
    remote(g_all.at[1 - core], g_all.at[1 - core], vs, vr, partner).wait_recv()
    nn = ((1,), (0,))

    def send(rows, weight):
        a, b = split(weight)
        u_out[rows, :] = dot(a, res[...], nn) + dot(b, res[...], nn)

    @pl.when(origin)
    def _():
        send(pl.ds(0, n), edit0[...])

    @pl.when(jnp.logical_not(origin))
    def _():
        c, d = split(edit0[...])

        def rows_part(i, _):
            rows = tile(i * 4 * piece, 4 * piece)
            g = jnp.concatenate([
                jnp.concatenate([g_all[0, 4 * i + s], g_all[1, 4 * i + s]], axis=1) for s in range(4)
            ], axis=0).astype(i32)
            scale = jnp.exp(g[:, n:n + 1].astype(f32) * STEP) * (1.0 / TOP)
            g = g[:, :n]
            high = lax.shift_right_arithmetic(g, 8)
            low = (g - high * 256).astype(f32).astype(bf16)
            high = high.astype(f32).astype(bf16)
            for lo in range(0, n, 256):
                hi = min(lo + 256, n)
                at = slice(lo, hi)
                a, b = inv_hi[at, :hi], inv_lo[at, :hi]
                big = dot(high[:, :hi], a, nt) + dot(high[:, :hi], b, nt)
                l_out[rows, at] = (big * 256.0 + dot(low[:, :hi], a, nt)) * scale
            a, b = split(l_out[rows, :])
            ends = jnp.concatenate([e_all[4 * i + s] for s in range(4)], axis=0).astype(f32)
            send(rows, ends - (dot(a, c, nn) + dot(a, d, nn) + dot(b, c, nn)))
            return 0

        lax.fori_loop(0, RING // 4, rows_part, 0)

    give_over.wait_send()
    for dz in range(1, RING):
        for copy in give(dz):
            copy.wait_send()
    pair.wait_send()
    for t in range(UNITS):
        hand_over(core, t).wait_send()

    @pl.when(origin)
    def _():
        for t in range(UNITS):
            if t == 0:
                @pl.when(core == 1)
                def _():
                    scatter(0, 0).wait_send()
            else:
                scatter(t, 0).wait_send()
            for dz in range(1, RING):
                scatter(t, dz).wait_send()

    for step in (1, 2, 3):
        token_first(step).wait_send()
        for s in range(2):
            token_row(s, step).wait_send()
            if step != 2:
                block_row(s, step).wait_send()

    @pl.when(core != mine)
    def _():
        token_first(0).wait_send()

    @pl.when(holder)
    def _():
        for step in (1, 2, 3):
            for half in range(2):
                block_first(half, step).wait_send()
            for j in range(COLS):
                token_column(j, step).wait_send()
                if step != 2:
                    block_column(j, step).wait_send()

    for s in range(2):
        for part in range(2):
            onward_row(s, part).wait_send()

            @pl.when(away(s) == (1, 3)[part])
            def _(s=s, part=part):
                for j in range(COLS):
                    onward_column(s, j, part).wait_send()

    def sent(j, _):
        weight_copy(j).wait_send()
        return 0

    lax.fori_loop(0, 2 * tiles, sent, 0)

    def ring_sent(u, _):
        for hop in range(4):
            far(u, hop).wait_send()
            if hop < 3:
                near(u, hop).wait_send()
        return 0

    lax.fori_loop(0, UNITS, ring_sent, 0)


def split(a):
    whole = a.astype(bf16)
    return whole, (a - whole.astype(f32)).astype(bf16)


def whole_call(tok, wg, wu, lengths, raw, regular, res):
    lanes, depth = tok.shape
    width = wg.shape[1]
    piece = width // RING
    rows = 2 * piece + 16
    n, blocks, facts = width, 2 * UNITS, 8 * 2 * RING
    dma = pltpu.SemaphoreType.DMA
    vmem = pl.BlockSpec(memory_space=pltpu.VMEM)
    tiles = 2 * width // 128
    return pl.pallas_call(
        whole_kernel,
        out_shape=[jax.ShapeDtypeStruct((n, n), f32), jax.ShapeDtypeStruct((n, res.shape[1]), f32)],
        in_specs=[pl.BlockSpec(memory_space=pl.ANY)] * 3 + [vmem] * 4,
        out_specs=[vmem] * 2,
        scratch_shapes=[
            pltpu.VMEM((lanes, depth), bf16),
            pltpu.VMEM((depth, width), bf16),
            pltpu.VMEM((depth, width), bf16),
            pltpu.VMEM((2, RING, 8, 128), f32),
            pltpu.VMEM((UNITS, 2, lanes, depth), bf16),
            pltpu.VMEM((2, 2 * width, depth), bf16),
            pltpu.VMEM((UNITS, 2 * width, lanes), f32),
            pltpu.VMEM((UNITS, 4, rows, lanes), i16),
            pltpu.VMEM((UNITS, 4, rows, lanes), i16),
            pltpu.VMEM((UNITS, 3, rows, lanes), i16),
            pltpu.VMEM((UNITS, 3, rows, lanes), i16),
            pltpu.VMEM((blocks, n, lanes), bf16),
            pltpu.VMEM((blocks, piece, lanes), bf16),
            pltpu.VMEM((blocks, facts, lanes), bf16),
            pltpu.VMEM((n, n), f32),
            pltpu.VMEM((128, 128), f32),
            pltpu.VMEM((128, 128), f32),
            pltpu.VMEM((piece, n), f32),
            pltpu.VMEM((n, facts), f32),
            pltpu.VMEM((piece, facts), f32),
            pltpu.VMEM((2, RING, piece, 512), i16),
            pltpu.VMEM((RING, piece, facts), bf16),
            pltpu.VMEM((n, n), bf16),
            pltpu.VMEM((n, n), bf16),
            dma((3,)), dma((RING - 1,)), dma((RING - 1,)), dma, dma,
            dma((4,)), dma((2, 3)), dma((COLS, 3)), dma((UNITS, 2)), dma((tiles,)), dma((tiles,)),
            dma((UNITS, 4)), dma((UNITS, 4)), dma((UNITS, 3)), dma((UNITS, 3)),
            dma, dma, dma((UNITS, RING)), dma, dma((RING - 1,)), dma((RING,)),
            dma((2, 3)), dma((2, 3)), dma((COLS, 3)), dma((UNITS, 2)),
            dma((2, 2)), dma((2, COLS)), dma((UNITS, 2, 2)), dma((UNITS,)), dma((UNITS,)),
            dma((RING - 1,)), dma((RING - 1,)), dma((RING - 1,)), dma((RING - 1,)), dma, dma,
        ],
        compiler_params=pltpu.CompilerParams(collective_id=0, has_side_effects=True, vmem_limit_bytes=60 << 20),
        name="panel_edit",
    )(tok, wg, wu, lengths, raw, regular, res)


def on_device(tokens_in, gate_weight, up_weight, doc_lengths, subject_raw, residuals, regular):
    return tuple(whole_call(tokens_in, gate_weight, up_weight, doc_lengths, subject_raw, regular, residuals))


def solution(mesh):
    return jax.shard_map(
        on_device,
        mesh=mesh,
        in_specs=(
            P(("row", "col"), "doc"),
            P("doc", ("row", "col")),
            P("doc", ("row", "col")),
            P("doc", None),
            P("doc", None),
            P(None, "doc"),
            P(),
        ),
        out_specs=(P(("row", "col"), None), P(("row", "col"), "doc")),
        check_vma=False,
    )
```
